512 devices in a mesh: row: 32 (over x, z_lo, core), col: 16 (over z_hi, y).
Axes of the slice: x: 4, y: 4, z: 16 (z_hi: 4, z_lo: 4; z = z_hi * 4 + z_lo), core: 2. Of those that a mesh axis runs over, the one named last changes fastest.
Arguments:
- tensor: float32 [512, 512, 256], P('row', 'col'), may hold values from -6 to 6
- factor_b: float32 [512, 32], P(('col', 'row')), may hold values from -170 to 170, as said below
- initial_third_factor: float32 [256, 32], replicated, may hold values from -170 to 170, as said below
Outputs:
- new_a: float32 [512, 32], P(('row', 'col'))
- new_b: float32 [512, 32], P(('col', 'row'))
- new_c: float32 [256, 32], replicated
- weights: float32 [32], replicated
The draws below stay inside these ranges and needn't reach their ends.
Inputs may be any that keep to these rules, and one draw needn't show every extreme that they name: `factor_b`: row scales rise along the rows and vary from row to row; columns are correlated. `initial_third_factor`: row scales rise along the rows and vary from row to row; columns are correlated.
All inputs are finite; a program needn't handle non-finite values.
Results may differ from the reference program's by a relative error of at most 0.0001.
Values sent between devices are 32-bit elements; how exact they have to be, the bound alone decides.
A program may use at most 64 MiB of HBM per device.

```python
import math
import jax
import jax.numpy as jnp
from jax import lax

R = 32
K = 256
SWEEPS = 1
I = 512
J = 512


def shape_rows(common, own, scales, rows):
    place = jnp.arange(rows, dtype=jnp.float32) / rows
    return (0.6 * common + 0.8 * own) * scales[:, None] * (1.0 + 2.0 * place)[:, None]


def draw_factor_b(key, part):
    key = jax.random.fold_in(key, 11)
    first, second, third = jax.random.split(key, 3)
    common = jnp.clip(jax.random.normal(first, (J, 1), jnp.float32), -4.0, 4.0)
    own = jnp.clip(jax.random.normal(second, (J, R), jnp.float32), -4.0, 4.0)
    scales = jnp.exp(jax.random.uniform(third, (J,), jnp.float32, 0.0, math.log(10.0)))
    return shape_rows(common, own, scales, J)


def draw_initial_third_factor(key, part):
    key = jax.random.fold_in(key, 13)
    first, second, third = jax.random.split(key, 3)
    common = jnp.clip(jax.random.normal(first, (K, 1), jnp.float32), -4.0, 4.0)
    own = jnp.clip(jax.random.normal(second, (K, R), jnp.float32), -4.0, 4.0)
    scales = jnp.exp(jax.random.uniform(third, (K,), jnp.float32, 0.0, math.log(10.0)))
    return shape_rows(common, own, scales, K)


def block_scale(stream_key, extent, pieces, smallest, high):
    loudness, own = 1.0, jax.random.fold_in(stream_key, 6)
    for dim, parts in pieces:
        draws = jnp.exp(jax.random.uniform(jax.random.fold_in(own, dim), (parts,), jnp.float32, smallest / len(pieces), high / len(pieces)))
        loudness = loudness * jnp.repeat(draws, extent[dim] // parts).reshape([-1 if axis == dim else 1 for axis in range(len(extent))])
    return loudness


def scatter_about(stream_key, shape, scale, limit, cuts=(), kind=jnp.bfloat16):
    result = scale * jax.random.normal(stream_key, shape, jnp.float32)
    if cuts:
        result = result * block_scale(stream_key, shape, cuts, -0.22, 0.18)
    return jnp.clip(result, -limit, limit).astype(kind)


def setup_inputs(seed: int = 0) -> dict:
    keys = jax.random.split(jax.random.key(seed), 4)
    return {
        "tensor": scatter_about(keys[0], (I, J, K), 1.0, 6.0, ((0, 32), (1, 16)), jnp.float32),
        "factor_b": draw_factor_b(jax.random.fold_in(keys[3], 71), 0),
        "initial_third_factor": draw_initial_third_factor(jax.random.fold_in(keys[3], 71), 0),
    }


HI = lax.Precision.HIGHEST
EPS = 1e-05
RIDGE_PENALTY = 0.05

def solve_mode(m_rows, left_factor_gram, right_factor_gram):
    decomposition_rank = left_factor_gram.shape[0]
    hadamard_gram = left_factor_gram * right_factor_gram
    hadamard_gram = hadamard_gram + RIDGE_PENALTY * (jnp.trace(hadamard_gram) / decomposition_rank) * jnp.eye(decomposition_rank, dtype=jnp.float32)
    lower_cholesky = jnp.linalg.cholesky(hadamard_gram)
    return jax.scipy.linalg.cho_solve((lower_cholesky, True), m_rows.T).T

def normalise(factor):
    count = factor.shape[0]
    norms = jnp.sqrt(lax.optimization_barrier(jnp.sum(factor * factor, axis=0)) / count + EPS)
    scaled = factor / norms
    gram = jnp.dot(scaled.T.astype(jnp.float32), scaled.astype(jnp.float32), precision=HI, preferred_element_type=jnp.float32) / count
    return (scaled, gram, norms)

def reference(tensor, factor_b, initial_third_factor):
    nrow_i, nrow_j, depth = tensor.shape
    flat = tensor.reshape(nrow_i * nrow_j, depth)
    b_full = factor_b
    c_full = initial_third_factor
    gram_b = jnp.dot(b_full.T.astype(jnp.float32), b_full.astype(jnp.float32), precision=HI, preferred_element_type=jnp.float32) / nrow_j
    gram_c = jnp.dot(c_full.T.astype(jnp.float32), c_full.astype(jnp.float32), precision=HI, preferred_element_type=jnp.float32) / depth
    a_full = jnp.zeros((nrow_i, b_full.shape[1]), jnp.float32)
    weights = jnp.zeros((b_full.shape[1],), jnp.float32)
    for sweep in range(SWEEPS):
        projected = jnp.dot(flat.astype(jnp.float32), c_full.astype(jnp.float32), precision=HI, preferred_element_type=jnp.float32)
        projected = projected.reshape(nrow_i, nrow_j, -1)
        m_one = jnp.einsum('ijr,jr->ir', projected, b_full, precision=HI)
        a_full, gram_a, norms = normalise(solve_mode(m_one, gram_b, gram_c))
        m_two = jnp.einsum('ijr,ir->jr', projected, a_full, precision=HI)
        b_full, gram_b, norms = normalise(solve_mode(m_two, gram_a, gram_c))
        khatri = (a_full[:, None, :] * b_full[None, :, :]).reshape(nrow_i * nrow_j, -1)
        third_mode_product = lax.dot_general(flat.astype(jnp.float32), khatri.astype(jnp.float32), (((0,), (0,)), ((), ())), precision=HI, preferred_element_type=jnp.float32)
        c_full, gram_c, norms = normalise(solve_mode(third_mode_product, gram_a, gram_b))
        weights = norms / jnp.sqrt(jnp.float32(nrow_i * nrow_j))
    return (a_full, b_full, c_full, weights)
```

```python
import functools
import itertools

import jax
import jax.numpy as jnp
from jax import lax
from jax.experimental import pallas as pl
from jax.experimental.pallas import tpu as pltpu
from jax.sharding import PartitionSpec as P

HI = lax.Precision.HIGHEST
EPS = 1e-05
RIDGE_PENALTY = 0.05
MESH = pl.DeviceIdType.MESH
F32 = jnp.float32
RANK = 32
SIZES = {"x": 4, "z_lo": 4, "core": 2, "z_hi": 4, "y": 4}
GROUPS = {
    "row": ("x", "z_lo", "core"),
    "z": ("z_hi", "z_lo"),
    "xyc": ("x", "y", "core"),
    "y": ("y",),
    "z_hi": ("z_hi",),
}


def iota(shape, dim):
    return lax.broadcasted_iota(jnp.int32, shape, dim)


def dot(a, b):
    return lax.dot_general(a, b, (((1,), (0,)), ((), ())), precision=HI, preferred_element_type=F32)


def gram(a):
    return lax.dot_general(a, a, (((0,), (0,)), ((), ())), precision=HI, preferred_element_type=F32)


def roll(a, by):
    return pltpu.roll(a, by, a.ndim - 1)


def position():
    row, col = lax.axis_index("row"), lax.axis_index("col")
    return {"x": row // 8, "z_lo": (row // 2) % 4, "core": row % 2, "z_hi": col // 4, "y": col % 4}


def device(place):
    return {
        "row": (place["x"] * 4 + place["z_lo"]) * 2 + place["core"],
        "col": place["z_hi"] * 4 + place["y"],
    }


def steps_of(group):
    dims = GROUPS[group]
    steps = [s for s in itertools.product(*[range(SIZES[d]) for d in dims]) if any(s)]
    far = {"x": 1, "y": 1, "z_lo": 1, "core": 0, "z_hi": 4}

    def hops(step):
        return sum(far[d] * min(s, SIZES[d] - s) for d, s in zip(dims, step))

    return [dict(zip(dims, s)) for s in sorted(steps, key=hops, reverse=True)]


def moved(place, step):
    out = dict(place)
    for d, s in step.items():
        if s:
            out[d] = (place[d] + s) % SIZES[d]
    return out


def index_in(group, place):
    index = 0
    for d in GROUPS[group]:
        index = index * SIZES[d] + place[d]
    return index


def lane_group(shape):
    return iota(shape, len(shape) - 1) // RANK


def eye_rep():
    return jnp.where(iota((RANK, 128), 0) == iota((RANK, 128), 1) % RANK, 1.0, 0.0).astype(F32)


def fold(a):
    a = a + roll(a, 64)
    return a + roll(a, 32)


def halves_gram(h):
    lanes = iota((RANK, 128), 1)
    t = jnp.where(lanes < 64, h[0:32, :], h[64:96, :])
    return t + roll(t, 64)


def quarters_gram(h):
    g = lane_group((RANK, 128))
    t = jnp.where(g == 0, h[0:32, :], jnp.where(g == 1, h[32:64, :], jnp.where(g == 2, h[64:96, :], h[96:128, :])))
    return fold(t)


def pack_square(m):
    g = lane_group((8, 128))
    return jnp.where(g == 0, m[0:8], jnp.where(g == 1, m[8:16], jnp.where(g == 2, m[16:24], m[24:32])))


def unpack_square(p):
    g = lane_group((8, 128))
    return jnp.concatenate([fold(jnp.where(g == q, p, 0.0)) for q in range(4)], axis=0)


def inverse(s):
    width, block = 128, 8
    rows, lanes = iota((RANK, width), 0), iota((RANK, width), 1)
    a = jnp.where(lanes < RANK, s, eye_rep())
    for k in range(0, RANK, block):
        c = [jnp.broadcast_to(a[:, k + j : k + j + 1], (RANK, width)) for j in range(block)]
        r = [a[k + j : k + j + 1, :] for j in range(block)]
        p = [[c[j][k + i : k + i + 1, :] for j in range(block)] for i in range(block)]
        for i in range(block):
            ip = 1.0 / p[i][i]
            r[i] = r[i] * ip
            for j in range(i + 1, block):
                p[i][j] = p[i][j] * ip
            for other in range(block):
                if other != i:
                    f = p[other][i]
                    r[other] = r[other] - f * r[i]
                    for j in range(i + 1, block):
                        p[other][j] = p[other][j] - f * p[i][j]
        u = c[0] * r[0]
        for j in range(1, block):
            u = u + c[j] * r[j]
        new = a - u
        pieces = [new[i : i + block] for i in range(0, RANK, block)]
        pieces[k // block] = jnp.concatenate(r, axis=0)
        a = jnp.concatenate(pieces, axis=0)
    return jnp.where(lanes < RANK, roll(a, 32), a)


def solver(gram_u, gram_w):
    eye = eye_rep()
    v = gram_u * gram_w
    trace = jnp.sum(jnp.sum(v * eye, axis=0, keepdims=True), axis=1, keepdims=True) / 4.0
    scale = RANK / trace
    return inverse(v * scale + RIDGE_PENALTY * eye) * scale


def scales(h, count):
    masked = h * eye_rep()
    along = 1.0 / jnp.sqrt(jnp.sum(masked, axis=0, keepdims=True) / count + EPS)
    down = 1.0 / jnp.sqrt(jnp.sum(masked, axis=1, keepdims=True) / 4.0 / count + EPS)
    return along, down, h * along * down / count


def kernel(tensor_hbm, b_hbm, c_hbm, a_out, b_out, c_out, w_out,
           x, c_in, b_in, y_i, y_j, x_t, b_send, b_rows, b_far, g_send, g_all,
           m1_send, m1_y, m1_zh, a_send, a_all, m2_send, m2_all, m3_send, m3_parts, m3z_send, m3_z, m3_done_send, m3_done,
           hb_send, hb_y, hbz_send, hb_zh, a_rows, b_packed, local, sent, got):
    place = position()
    at = {g: index_in(g, place) for g in GROUPS}
    total_i, total_j, depth = 512, 512, 256

    loads = [
        pltpu.make_async_copy(b_hbm, b_in, local.at[0]),
        pltpu.make_async_copy(c_hbm, c_in, local.at[1]),
        pltpu.make_async_copy(tensor_hbm, x, local.at[2]),
    ]
    for load in loads:
        load.start()

    barrier = pltpu.get_barrier_semaphore()
    greeted = []
    for group in ("row", "z", "xyc"):
        for step in steps_of(group):
            step = {d: s for d, s in step.items() if s}
            if step not in greeted:
                greeted.append(step)
    for step in greeted:
        pl.semaphore_signal(barrier, inc=1, device_id=device(moved(place, step)), device_id_type=MESH)

    rounds = itertools.count()

    def exchange(group, source, buffer):
        k = next(rounds)
        steps = steps_of(group)
        for step in steps:
            there = moved(place, step)
            src = source(there) if callable(source) else source
            pltpu.make_async_remote_copy(
                src_ref=src, dst_ref=buffer.at[at[group]], send_sem=sent.at[k], recv_sem=got.at[k],
                device_id=device(there), device_id_type=MESH,
            ).start()
        n = len(steps)
        span = buffer.at[pl.ds(0, n)]
        return pltpu.make_async_copy(span, span, got.at[k]), pltpu.make_async_copy(span, span, sent.at[k])

    loads[0].wait()
    b4 = jnp.concatenate([b_in[...]] * 4, axis=1)
    b_send[...] = b4
    b_rows[at["row"]] = b4
    b_far[at["z"]] = b4
    loads[1].wait()
    c4 = jnp.concatenate([c_in[...]] * 4, axis=1)
    gram_c = gram(c4)[0:32, :] / depth
    loads[2].wait()
    wide = lane_group((depth, 128))
    y = jnp.zeros((128, 128), F32)
    for q in range(4):
        part = x[:, 8 * q : 8 * q + 8, :].reshape(128, depth)
        y = y + dot(part, jnp.where(wide == q, c4, 0.0))
        x_t[:, 128 * q : 128 * q + 128] = part.T
    y = y.reshape(16, 8, 128)
    y_i[...] = y
    for s in range(8):
        y_j[s] = y[:, s, :]

    pl.semaphore_wait(barrier, len(greeted))

    pending = []

    def go(*args):
        arrive, leave = exchange(*args)
        pending.append(leave)
        return arrive

    b_near_in = go("row", b_send, b_rows)
    b_far_in = go("z", b_send, b_far)

    b_near_in.wait()
    near = b_rows[...].reshape(32, 128)
    b_pack = pack_square(near)
    m1 = y_j[0] * b_pack[0:1]
    for s in range(1, 8):
        m1 = m1 + y_j[s] * b_pack[s : s + 1]
    m1 = fold(m1)
    lanes8 = iota((8, 128), 1)
    m1_pack = jnp.where(lanes8 < 64, m1[0:8], m1[8:16])
    m1_send[0] = m1_pack
    m1_y[at["y"]] = m1_pack
    m1_y_in = go("y", m1_send.at[0], m1_y)

    m1_y_in.wait()
    m1 = m1_y[0] + m1_y[1] + m1_y[2] + m1_y[3]
    m1_send[1] = m1
    m1_zh[at["z_hi"]] = m1
    m1_zh_in = go("z_hi", m1_send.at[1], m1_zh)

    b_far_in.wait()
    far = b_far[...].reshape(16, 128)
    far = jnp.where(lanes8 < 64, far[0:8], far[8:16])
    g_send[...] = far
    g_all[at["xyc"]] = far
    g_in = go("xyc", g_send, g_all)
    g_in.wait()
    gram_b = halves_gram(gram(g_all[...].reshape(256, 128))) / total_j
    solve_a = solver(gram_b, gram_c)
    lanes32 = iota((RANK, 128), 1)
    zero = jnp.zeros((RANK, 128), F32)
    solve_halves = jnp.concatenate(
        [jnp.where(lanes32 < 64, solve_a, 0.0), zero, jnp.where(lanes32 < 64, 0.0, solve_a), zero], axis=0
    )

    m1_zh_in.wait()
    m1 = m1_zh[0] + m1_zh[1] + m1_zh[2] + m1_zh[3]
    a_pack = dot(m1, solve_halves)
    a_send[...] = a_pack
    a_all[at["row"]] = a_pack
    a_in = go("row", a_send, a_all)
    turned = roll(a_pack, 64)
    a_own = jnp.concatenate([jnp.where(lanes8 < 64, a_pack, turned), jnp.where(lanes8 < 64, turned, a_pack)], axis=0)
    a_rows[...] = a_own
    m2 = y_i[0] * a_own[0:1]
    for i in range(1, 16):
        m2 = m2 + y_i[i] * a_own[i : i + 1]
    m2_send[...] = m2
    m2_all[at["row"]] = m2
    m2_in = go("row", m2_send, m2_all)

    a_in.wait()
    gram_h = halves_gram(gram(a_all[...].reshape(256, 128)))
    a_along, _, gram_a = scales(gram_h, total_i)
    solve_b = solver(gram_a, gram_c)
    group32 = lane_group((RANK, 128))
    solve_quarters = jnp.concatenate([jnp.where(group32 == q, solve_b, 0.0) for q in range(4)], axis=0)

    m2_in.wait()
    m2 = jnp.sum(m2_all[...], axis=0) * a_along
    b_pack = dot(m2, solve_quarters)
    b_packed[...] = b_pack
    scaled_b = b_pack * a_along
    khatri = (a_own[:, None, :] * scaled_b[None, :, :]).reshape(128, 128)
    group128 = lane_group((128, 128))
    khatri = jnp.concatenate([jnp.where(group128 == q, khatri, 0.0) for q in range(4)], axis=0)
    m3 = dot(x_t[...], khatri)
    m3_send[...] = m3.reshape(32, 8, 128)
    m3_parts[at["xyc"]] = m3_send[at["xyc"]]
    m3_in = go("xyc", lambda there: m3_send.at[index_in("xyc", there)], m3_parts)

    hb = pack_square(quarters_gram(gram(b_pack)))
    hb_send[...] = hb
    hb_y[at["y"]] = hb
    hb_y_in = go("y", hb_send, hb_y)

    m3_in.wait()
    m3 = fold(jnp.sum(m3_parts[...], axis=0))
    m3z_send[...] = m3
    m3_z[at["z"]] = m3
    m3z_in = go("z", m3z_send, m3_z)

    hb_y_in.wait()
    hb = hb_y[0] + hb_y[1] + hb_y[2] + hb_y[3]
    hbz_send[...] = hb
    hb_zh[at["z_hi"]] = hb
    hb_zh_in = go("z_hi", hbz_send, hb_zh)

    a_out[...] = (a_rows[pl.ds(lax.axis_index("col"), 1), :] * a_along)[:, 0:RANK]

    m3z_in.wait()
    m3 = jnp.sum(m3_z[...], axis=0)
    m3_done_send[...] = m3
    m3_done[at["xyc"]] = m3
    done_in = go("xyc", m3_done_send, m3_done)

    hb_zh_in.wait()
    hb = unpack_square(hb_zh[0] + hb_zh[1] + hb_zh[2] + hb_zh[3])
    b_along, b_down, gram_b = scales(hb, total_j)
    row = at["row"]
    own_b = b_packed[pl.ds(row % 8, 1), :]
    own_b = fold(jnp.where(lane_group((1, 128)) == row // 8, own_b, 0.0))
    b_out[...] = (own_b * b_along)[:, 0:RANK]
    solve_c = solver(gram_a, gram_b) * b_down

    done_in.wait()
    m3 = m3_done[...].reshape(256, 128)
    fresh = dot(m3[:, 0:RANK], solve_c)
    norms = jnp.sqrt(jnp.sum(fresh * fresh, axis=0, keepdims=True) / depth + EPS)
    c_out[...] = (fresh / norms)[:, 0:RANK]
    w_out[...] = norms[:, 0:RANK] / 512.0

    for leave in pending:
        leave.wait()


def per_device(tensor, factor_b, initial_third_factor):
    tile = (8, 128)
    vmem = lambda *shape: pltpu.VMEM(shape, F32)
    a, b, c, w = pl.pallas_call(
        kernel,
        out_shape=(
            jax.ShapeDtypeStruct((1, RANK), F32),
            jax.ShapeDtypeStruct((1, RANK), F32),
            jax.ShapeDtypeStruct((256, RANK), F32),
            jax.ShapeDtypeStruct((1, RANK), F32),
        ),
        in_specs=[pl.BlockSpec(memory_space=pl.ANY)] * 3,
        out_specs=[pl.BlockSpec(memory_space=pltpu.VMEM)] * 4,
        scratch_shapes=[
            vmem(16, 32, 256), vmem(256, RANK), vmem(1, RANK), vmem(16, *tile), vmem(8, 16, 128), vmem(256, 512),
            vmem(1, 128), vmem(32, 1, 128), vmem(16, 1, 128), vmem(*tile), vmem(32, *tile),
            vmem(2, *tile), vmem(4, *tile), vmem(4, *tile), vmem(*tile), vmem(32, *tile), vmem(*tile), vmem(32, *tile),
            vmem(32, *tile), vmem(32, *tile), vmem(*tile), vmem(16, *tile), vmem(*tile), vmem(32, *tile),
            vmem(*tile), vmem(4, *tile), vmem(*tile), vmem(4, *tile), vmem(16, 128), vmem(*tile),
            pltpu.SemaphoreType.DMA((3,)), pltpu.SemaphoreType.DMA((12,)), pltpu.SemaphoreType.DMA((12,)),
        ],
        compiler_params=pltpu.CompilerParams(
            collective_id=0, has_side_effects=True, vmem_limit_bytes=32 * 1024 * 1024
        ),
        name="als_sweep",
    )(tensor, factor_b, initial_third_factor)
    return a, b, c, w.reshape(RANK)


def solution(mesh):
    return jax.shard_map(
        per_device,
        mesh=mesh,
        in_specs=(P("row", "col", None), P(("col", "row"), None), P()),
        out_specs=(P(("row", "col"), None), P(("col", "row"), None), P(), P()),
        check_vma=False,
    )
```

```python
import functools
import itertools

import jax
import jax.numpy as jnp
from jax import lax
from jax.experimental import pallas as pl
from jax.experimental.pallas import tpu as pltpu
from jax.sharding import PartitionSpec as P

HI = lax.Precision.HIGHEST
EPS = 1e-05
RIDGE_PENALTY = 0.05
MESH = pl.DeviceIdType.MESH
F32 = jnp.float32
RANK = 32
SIZES = {"x": 4, "z_lo": 4, "core": 2, "z_hi": 4, "y": 4}
GROUPS = {
    "row": ("x", "z_lo", "core"),
    "z": ("z_hi", "z_lo"),
    "xyc": ("x", "y", "core"),
    "col": ("z_hi", "y"),
    "x_z": ("x", "z_lo"),
    "core": ("core",),
    "y": ("y",),
}


def iota(shape, dim):
    return lax.broadcasted_iota(jnp.int32, shape, dim)


def dot(a, b):
    return lax.dot_general(a, b, (((1,), (0,)), ((), ())), precision=HI, preferred_element_type=F32)


def gram(a):
    return lax.dot_general(a, a, (((0,), (0,)), ((), ())), precision=HI, preferred_element_type=F32)


def roll(a, by):
    return pltpu.roll(a, by, a.ndim - 1)


class Places:
    def __init__(self):
        row, col = lax.axis_index("row"), lax.axis_index("col")
        rem, div = lax.rem, lax.div
        self.own = {"x": div(row, 8), "z_lo": rem(div(row, 2), 4), "core": rem(row, 2), "z_hi": div(col, 4), "y": rem(col, 4)}
        self.weight = {"x": 8, "z_lo": 2, "core": 1, "z_hi": 4, "y": 1}
        self.known = {}

    def coordinate(self, dim, step):
        if (dim, step) not in self.known:
            there = lax.rem(self.own[dim] + step, SIZES[dim]) if step else self.own[dim]
            self.known[dim, step] = there, there * self.weight[dim]
        return self.known[dim, step]

    def device(self, step):
        at = {d: self.coordinate(d, step.get(d, 0))[1] for d in SIZES}
        return {"row": at["x"] + at["z_lo"] + at["core"], "col": at["z_hi"] + at["y"]}

    def index(self, group, step=None):
        index = 0
        for d in GROUPS[group]:
            index = index * SIZES[d] + self.coordinate(d, (step or {}).get(d, 0))[0]
        return index


def steps_of(group):
    dims = GROUPS[group]
    steps = [s for s in itertools.product(*[range(SIZES[d]) for d in dims]) if any(s)]
    return farthest_first([{d: n for d, n in zip(dims, s) if n} for s in steps])


def farthest_first(steps):
    far = {"x": 1, "y": 1, "z_lo": 1, "core": 0, "z_hi": 4}
    return sorted(steps, key=lambda step: sum(far[d] * min(n, SIZES[d] - n) for d, n in step.items()), reverse=True)


def lane_group(shape):
    return iota(shape, len(shape) - 1) // RANK


def eye_rep():
    return jnp.where(iota((RANK, 128), 0) == iota((RANK, 128), 1) % RANK, 1.0, 0.0).astype(F32)


def fold(a):
    a = a + roll(a, 64)
    return a + roll(a, 32)


def quarters_gram(h):
    g = lane_group((RANK, 128))
    t = jnp.where(g == 0, h[0:32, :], jnp.where(g == 1, h[32:64, :], jnp.where(g == 2, h[64:96, :], h[96:128, :])))
    return fold(t)


def pack_square(m):
    g = lane_group((8, 128))
    return jnp.where(g == 0, m[0:8], jnp.where(g == 1, m[8:16], jnp.where(g == 2, m[16:24], m[24:32])))


def pack_rows(m):
    g = lane_group((8, 128))
    low, high = (jnp.where(g % 2 == 1, pltpu.roll(half, 4, 0), half) for half in (m[0:8], m[8:16]))
    return jnp.where(g < 2, low, high)[0:4]


def by_quarter(m):
    g = lane_group((RANK, 128))
    return jnp.concatenate([jnp.where(g == q, m, 0.0) for q in range(4)], axis=0)


def inverse(s):
    width, block = 128, 8
    rows, lanes = iota((RANK, width), 0), iota((RANK, width), 1)
    a = jnp.where(lanes < RANK, s, eye_rep())
    for k in range(0, RANK, block):
        c = [jnp.broadcast_to(a[:, k + j : k + j + 1], (RANK, width)) for j in range(block)]
        r = [a[k + j : k + j + 1, :] for j in range(block)]
        p = [[c[j][k + i : k + i + 1, :] for j in range(block)] for i in range(block)]
        for i in range(block):
            ip = 1.0 / p[i][i]
            r[i] = r[i] * ip
            for j in range(i + 1, block):
                p[i][j] = p[i][j] * ip
            for other in range(block):
                if other != i:
                    f = p[other][i]
                    r[other] = r[other] - f * r[i]
                    for j in range(i + 1, block):
                        p[other][j] = p[other][j] - f * p[i][j]
        u = c[0] * r[0]
        for j in range(1, block):
            u = u + c[j] * r[j]
        new = a - u
        pieces = [new[i : i + block] for i in range(0, RANK, block)]
        pieces[k // block] = jnp.concatenate(r, axis=0)
        a = jnp.concatenate(pieces, axis=0)
    return jnp.where(lanes < RANK, roll(a, 32), a)


def solver(gram_u, gram_w):
    eye = eye_rep()
    v = gram_u * gram_w
    trace = jnp.sum(jnp.sum(v * eye, axis=0, keepdims=True), axis=1, keepdims=True) / 4.0
    scale = RANK / trace
    return inverse(v * scale + RIDGE_PENALTY * eye) * scale


def scales(h, count):
    masked = h * eye_rep()
    along = 1.0 / jnp.sqrt(jnp.sum(masked, axis=0, keepdims=True) / count + EPS)
    down = 1.0 / jnp.sqrt(jnp.sum(masked, axis=1, keepdims=True) / 4.0 / count + EPS)
    return along, h * along * down / count


def kernel(tensor_hbm, b_hbm, c_hbm, a_out, b_out, c_out, w_out,
           x, c_in, b_in, y_i, y_j, x_flat, b_send, b_rows, b_far, g_send, g_all,
           m1_send, m1_all, a_send, a_all, m2_send, m2_all, m2_half, m2_pair, m3_send, m3_parts, m3z_send, m3_z, m3_done_send, m3_done,
           hb_send, hb_far, hbx_send, hb_all, a_rows, local, sent, got, near):
    places = Places()
    at = {g: places.index(g) for g in GROUPS}
    total_i, total_j, depth = 512, 512, 256

    barrier = pltpu.get_barrier_semaphore()
    greeted = []
    for group in ("z", "xyc", "row"):
        for step in steps_of(group):
            if step not in greeted:
                greeted.append(step)
    for step in farthest_first(greeted):
        pl.semaphore_signal(barrier, inc=1, device_id=places.device(step), device_id_type=MESH)

    loads = [
        pltpu.make_async_copy(b_hbm, b_in, local.at[0]),
        pltpu.make_async_copy(c_hbm, c_in, local.at[1]),
        pltpu.make_async_copy(tensor_hbm, x, local.at[2]),
    ]
    for load in loads:
        load.start()

    rounds = itertools.count()
    pending = []

    def exchange(group, source, buffer):
        k = next(rounds)
        steps = steps_of(group)
        for step in steps:
            src = source(step) if callable(source) else source
            pltpu.make_async_remote_copy(
                src_ref=src, dst_ref=buffer.at[at[group]], send_sem=sent.at[k], recv_sem=got.at[k],
                device_id=places.device(step), device_id_type=MESH,
            ).start()
        n = len(steps)
        span = buffer.at[pl.ds(0, n)]
        return pltpu.make_async_copy(span, span, got.at[k]), pltpu.make_async_copy(span, span, sent.at[k])

    loads[0].wait()
    b4 = jnp.concatenate([b_in[...]] * 4, axis=1)
    b_send[...] = b4
    b_rows[at["row"]] = b4
    b_far[at["z"]] = b4
    loads[1].wait()
    c4 = jnp.concatenate([c_in[...]] * 4, axis=0).T
    gram_c = gram(c4)[0:32, :] / depth
    loads[2].wait()
    wide = lane_group((depth, 128))
    y = jnp.zeros((128, 128), F32)
    for q in range(4):
        part = x[:, 8 * q : 8 * q + 8, :].reshape(128, depth)
        y = y + dot(part, jnp.where(wide == q, c4, 0.0))
        x_flat[128 * q : 128 * q + 128, :] = part
    y = y.reshape(16, 8, 128)
    y_i[...] = y
    for s in range(8):
        y_j[s] = y[:, s, :]

    pl.semaphore_wait(barrier, len(greeted))

    def go(*args):
        arrive, leave = exchange(*args)
        pending.append(leave)
        return arrive

    b_near_in = go("row", b_send, b_rows)
    b_far_in = go("z", b_send, b_far)
    for step in steps_of("y"):
        pl.semaphore_signal(near, inc=1, device_id=places.device(step), device_id_type=MESH)

    b_near_in.wait()
    b_pack = pack_square(b_rows[...].reshape(32, 128))
    m1 = y_j[0] * b_pack[0:1]
    for s in range(1, 8):
        m1 = m1 + y_j[s] * b_pack[s : s + 1]
    m1 = pack_rows(fold(m1))
    m1_send[...] = m1
    m1_all[at["col"]] = m1
    pl.semaphore_wait(near, len(steps_of("y")))
    m1_in = go("col", m1_send, m1_all)

    b_far_in.wait()
    far = pack_rows(b_far[...].reshape(16, 128))
    g_send[...] = far
    g_all[at["xyc"]] = far
    g_in = go("xyc", g_send, g_all)
    g_in.wait()
    gram_b = quarters_gram(gram(g_all[...].reshape(128, 128))) / total_j
    solve_a = solver(gram_b, gram_c)
    solve_rows = jnp.concatenate([solve_a] * 4, axis=0)
    solve_a = by_quarter(solve_a)

    m1_in.wait()
    m1 = jnp.sum(m1_all[...], axis=0)
    m1 = jnp.concatenate([m1, m1], axis=0)
    a_pack = dot(m1, solve_a)[0:4]
    group8, upper = lane_group((8, 128)), iota((8, 128), 0) // 4
    m1 = jnp.concatenate([jnp.where(group8 == 2 * t + upper, m1, 0.0) for t in range(2)], axis=0)
    a_own = dot(m1, solve_rows)
    a_send[...] = a_pack
    a_all[at["row"]] = a_pack
    a_in = go("row", a_send, a_all)
    a_rows[...] = a_own
    m2 = y_i[0] * a_own[0:1]
    for i in range(1, 16):
        m2 = m2 + y_i[i] * a_own[i : i + 1]
    m2_send[...] = m2
    m2_all[at["x_z"]] = m2
    m2_in = go("x_z", m2_send, m2_all)

    m2_in.wait()
    m2 = jnp.sum(m2_all[...], axis=0)
    m2_half[...] = m2
    m2_pair[at["core"]] = m2
    m2_in = go("core", m2_half, m2_pair)

    a_in.wait()
    gram_h = quarters_gram(gram(a_all[...].reshape(128, 128)))
    a_along, gram_a = scales(gram_h, total_i)
    solve_b = by_quarter(solver(gram_a, gram_c))

    m2_in.wait()
    b_pack = dot((m2_pair[0] + m2_pair[1]) * a_along, solve_b)
    scaled_b = b_pack * a_along
    khatri = (a_own[:, None, :] * scaled_b[None, :, :]).reshape(128, 128).T
    khatri = jnp.concatenate([khatri[32 * q : 32 * q + 32] for q in range(4)], axis=1)
    m3 = dot(khatri, x_flat[...])
    m3_send[...] = m3.reshape(32, 1, 256)
    m3_parts[at["xyc"]] = m3_send[at["xyc"]]
    m3_in = go("xyc", lambda step: m3_send.at[places.index("xyc", step)], m3_parts)
    own = fold(jnp.where(lane_group((8, 128)) == at["row"] // 8, b_pack, 0.0))
    own = jnp.sum(jnp.where(iota((8, 128), 0) == at["row"] % 8, own, 0.0), axis=0, keepdims=True)
    hb_send[...] = own
    hb_far[at["z"]] = own
    hb_far_in = go("z", hb_send, hb_far)
    a_out[...] = (a_rows[pl.ds(at["col"], 1), :] * a_along)[:, 0:RANK]

    m3_in.wait()
    m3 = jnp.sum(m3_parts[...], axis=0)
    m3z_send[...] = m3
    m3_z[at["z"]] = m3
    m3z_in = go("z", m3z_send, m3_z)

    hb_far_in.wait()
    hb = pack_rows(hb_far[...].reshape(16, 128))
    hbx_send[...] = hb
    hb_all[at["xyc"]] = hb
    hb_in = go("xyc", hbx_send, hb_all)

    m3z_in.wait()
    m3 = jnp.sum(m3_z[...], axis=0)
    m3_done_send[...] = m3
    m3_done[at["xyc"]] = m3
    done_in = go("xyc", m3_done_send, m3_done)

    hb_in.wait()
    b_along, gram_b = scales(quarters_gram(gram(hb_all[...].reshape(128, 128))), total_j)
    b_out[...] = (hb_send[...] * b_along)[:, 0:RANK]
    solve_c = (solver(gram_a, gram_b) * b_along)[:, 0:RANK]

    done_in.wait()
    fresh = dot(solve_c, m3_done[...].reshape(RANK, depth))
    norms = jnp.sqrt(jnp.sum(fresh * fresh, axis=1, keepdims=True) / depth + EPS)
    c_out[...] = fresh / norms
    w_out[...] = jnp.sum(norms * eye_rep(), axis=0, keepdims=True)[:, 0:RANK] / 512.0

    for leave in pending:
        leave.wait()


def hand_over(*refs):
    copies = [pltpu.make_async_copy(refs[k], refs[4 + k], refs[8].at[k]) for k in range(4)]
    for copy in copies:
        copy.start()
    for copy in copies:
        copy.wait()


def per_device(tensor, factor_b, initial_third_factor):
    tile = (8, 128)
    vmem = lambda *shape: pltpu.VMEM(shape, F32)
    results = (
        jax.ShapeDtypeStruct((1, RANK), F32),
        jax.ShapeDtypeStruct((1, RANK), F32),
        jax.ShapeDtypeStruct((RANK, 256), F32),
        jax.ShapeDtypeStruct((1, RANK), F32),
    )
    ready = pl.pallas_call(
        kernel,
        out_shape=results,
        in_specs=[pl.BlockSpec(memory_space=pltpu.HBM)] * 3,
        out_specs=[pl.BlockSpec(memory_space=pltpu.VMEM)] * 4,
        scratch_shapes=[
            vmem(16, 32, 256), vmem(RANK, 256), vmem(1, RANK), vmem(16, *tile), vmem(8, 16, 128), vmem(512, 256),
            vmem(1, 128), vmem(32, 1, 128), vmem(16, 1, 128), vmem(4, 128), vmem(32, 4, 128),
            vmem(4, 128), vmem(16, 4, 128), vmem(4, 128), vmem(32, 4, 128),
            vmem(*tile), vmem(16, *tile), vmem(*tile), vmem(2, *tile),
            vmem(32, 1, 256), vmem(32, 1, 256), vmem(1, 256), vmem(16, 1, 256), vmem(1, 256), vmem(32, 1, 256),
            vmem(1, 128), vmem(16, 1, 128), vmem(4, 128), vmem(32, 4, 128), vmem(16, 128),
            pltpu.SemaphoreType.DMA((3,)), pltpu.SemaphoreType.DMA((12,)), pltpu.SemaphoreType.DMA((12,)),
            pltpu.SemaphoreType.REGULAR,
        ],
        compiler_params=pltpu.CompilerParams(
            collective_id=0, has_side_effects=True, vmem_limit_bytes=60 * 1024 * 1024
        ),
        name="als_sweep",
    )(tensor, factor_b, initial_third_factor.T)
    a, b, c, w = pl.pallas_call(
        hand_over,
        out_shape=results,
        in_specs=[pl.BlockSpec(memory_space=pltpu.VMEM)] * 4,
        out_specs=[pl.BlockSpec(memory_space=pltpu.HBM)] * 4,
        scratch_shapes=[pltpu.SemaphoreType.DMA((4,))],
        name="hand_over",
    )(*ready)
    return a, b, c.T, w.reshape(RANK)


def solution(mesh):
    return jax.shard_map(
        per_device,
        mesh=mesh,
        in_specs=(P("row", "col", None), P(("col", "row"), None), P()),
        out_specs=(P(("row", "col"), None), P(("col", "row"), None), P(), P()),
        check_vma=False,
    )
```

```python
import functools
import itertools

import jax
import jax.numpy as jnp
from jax import lax
from jax.experimental import pallas as pl
from jax.experimental.pallas import tpu as pltpu
from jax.sharding import PartitionSpec as P

HI = lax.Precision.HIGHEST
EPS = 1e-05
RIDGE_PENALTY = 0.05
MESH = pl.DeviceIdType.MESH
F32 = jnp.float32
RANK = 32
SIZES = {"x": 4, "z_lo": 4, "core": 2, "z_hi": 4, "y": 4}
GROUPS = {
    "row": ("x", "z_lo", "core"),
    "z": ("z_hi", "z_lo"),
    "xyc": ("x", "y", "core"),
    "col": ("z_hi", "y"),
    "x_z": ("x", "z_lo"),
    "core": ("core",),
    "y": ("y",),
}


def iota(shape, dim):
    return lax.broadcasted_iota(jnp.int32, shape, dim)


def dot(a, b):
    return lax.dot_general(a, b, (((1,), (0,)), ((), ())), precision=HI, preferred_element_type=F32)


def gram(a):
    return lax.dot_general(a, a, (((0,), (0,)), ((), ())), precision=HI, preferred_element_type=F32)


def roll(a, by):
    return pltpu.roll(a, by, a.ndim - 1)


class Places:
    def __init__(self):
        row, col = lax.axis_index("row"), lax.axis_index("col")
        rem, div = lax.rem, lax.div
        self.own = {"x": div(row, 8), "z_lo": rem(div(row, 2), 4), "core": rem(row, 2), "z_hi": div(col, 4), "y": rem(col, 4)}
        self.weight = {"x": 8, "z_lo": 2, "core": 1, "z_hi": 4, "y": 1}
        self.known = {}

    def coordinate(self, dim, step):
        if (dim, step) not in self.known:
            there = lax.rem(self.own[dim] + step, SIZES[dim]) if step else self.own[dim]
            self.known[dim, step] = there, there * self.weight[dim]
        return self.known[dim, step]

    def device(self, step):
        at = {d: self.coordinate(d, step.get(d, 0))[1] for d in SIZES}
        return {"row": at["x"] + at["z_lo"] + at["core"], "col": at["z_hi"] + at["y"]}

    def index(self, group, step=None):
        index = 0
        for d in GROUPS[group]:
            index = index * SIZES[d] + self.coordinate(d, (step or {}).get(d, 0))[0]
        return index


def steps_of(group):
    dims = GROUPS[group]
    steps = [s for s in itertools.product(*[range(SIZES[d]) for d in dims]) if any(s)]
    return farthest_first([{d: n for d, n in zip(dims, s) if n} for s in steps])


def farthest_first(steps):
    far = {"x": 1, "y": 1, "z_lo": 1, "core": 0, "z_hi": 4}
    return sorted(steps, key=lambda step: sum(far[d] * min(n, SIZES[d] - n) for d, n in step.items()), reverse=True)


def lane_group(shape):
    return iota(shape, len(shape) - 1) // RANK


def eye_rep():
    return jnp.where(iota((RANK, 128), 0) == iota((RANK, 128), 1) % RANK, 1.0, 0.0).astype(F32)


def fold(a):
    a = a + roll(a, 64)
    return a + roll(a, 32)


def quarters_gram(h):
    g = lane_group((RANK, 128))
    t = jnp.where(g == 0, h[0:32, :], jnp.where(g == 1, h[32:64, :], jnp.where(g == 2, h[64:96, :], h[96:128, :])))
    return fold(t)


def pack_square(m):
    g = lane_group((8, 128))
    return jnp.where(g == 0, m[0:8], jnp.where(g == 1, m[8:16], jnp.where(g == 2, m[16:24], m[24:32])))


def pack_rows(m):
    g = lane_group((8, 128))
    low, high = (jnp.where(g % 2 == 1, pltpu.roll(half, 4, 0), half) for half in (m[0:8], m[8:16]))
    return jnp.where(g < 2, low, high)[0:4]


def by_quarter(m):
    g = lane_group((RANK, 128))
    return jnp.concatenate([jnp.where(g == q, m, 0.0) for q in range(4)], axis=0)


def inverse(s):
    width, block = 128, 8
    rows, lanes = iota((RANK, width), 0), iota((RANK, width), 1)
    a = jnp.where(lanes < RANK, s, eye_rep())
    for k in range(0, RANK, block):
        c = [jnp.broadcast_to(a[:, k + j : k + j + 1], (RANK, width)) for j in range(block)]
        r = [a[k + j : k + j + 1, :] for j in range(block)]
        p = [[c[j][k + i : k + i + 1, :] for j in range(block)] for i in range(block)]
        for i in range(block):
            ip = 1.0 / p[i][i]
            r[i] = r[i] * ip
            for j in range(i + 1, block):
                p[i][j] = p[i][j] * ip
            for other in range(block):
                if other != i:
                    f = p[other][i]
                    r[other] = r[other] - f * r[i]
                    for j in range(i + 1, block):
                        p[other][j] = p[other][j] - f * p[i][j]
        u = c[0] * r[0]
        for j in range(1, block):
            u = u + c[j] * r[j]
        new = a - u
        pieces = [new[i : i + block] for i in range(0, RANK, block)]
        pieces[k // block] = jnp.concatenate(r, axis=0)
        a = jnp.concatenate(pieces, axis=0)
    return jnp.where(lanes < RANK, roll(a, 32), a)


def solver(gram_u, gram_w):
    eye = eye_rep()
    v = gram_u * gram_w
    trace = jnp.sum(jnp.sum(v * eye, axis=0, keepdims=True), axis=1, keepdims=True) / 4.0
    return inverse(v + (RIDGE_PENALTY / RANK) * trace * eye)


def scales(h, count):
    masked = h * eye_rep()
    along = 1.0 / jnp.sqrt(jnp.sum(masked, axis=0, keepdims=True) / count + EPS)
    down = 1.0 / jnp.sqrt(jnp.sum(masked, axis=1, keepdims=True) / 4.0 / count + EPS)
    return along, h * along * down / count


def kernel(tensor_hbm, b_hbm, c_hbm, a_out, b_out, c_out, w_out,
           x, c_in, b_in, y_i, y_j, x_flat, b_send, b_rows, b_far, g_send, g_all,
           m1_send, m1_all, a_send, a_all, m2_send, m2_all, m2_half, m2_pair, m3_send, m3_parts, m3z_send, m3_z, m3_done_send, m3_done,
           hb_send, hb_far, hbx_send, hb_all, a_rows, local, sent, got, near):
    places = Places()
    at = {g: places.index(g) for g in GROUPS}
    total_i, total_j, depth = 512, 512, 256

    barrier = pltpu.get_barrier_semaphore()
    greeted = []
    for group in ("z", "row", "y"):
        for step in steps_of(group):
            if step not in greeted:
                greeted.append(step)
    for step in farthest_first(greeted):
        pl.semaphore_signal(barrier, inc=1, device_id=places.device(step), device_id_type=MESH)

    loads = [
        pltpu.make_async_copy(b_hbm, b_in, local.at[0]),
        pltpu.make_async_copy(c_hbm, c_in, local.at[1]),
        pltpu.make_async_copy(tensor_hbm, x, local.at[2]),
    ]
    for load in loads:
        load.start()

    rounds = itertools.count()
    pending = []

    def exchange(group, source, buffer):
        k = next(rounds)
        steps = steps_of(group)
        for step in steps:
            src = source(step) if callable(source) else source
            pltpu.make_async_remote_copy(
                src_ref=src, dst_ref=buffer.at[at[group]], send_sem=sent.at[k], recv_sem=got.at[k],
                device_id=places.device(step), device_id_type=MESH,
            ).start()
        n = len(steps)
        span = buffer.at[pl.ds(0, n)]
        return pltpu.make_async_copy(span, span, got.at[k]), pltpu.make_async_copy(span, span, sent.at[k])

    loads[0].wait()
    b4 = jnp.concatenate([b_in[...]] * 4, axis=1)
    b_send[...] = b4
    b_rows[at["row"]] = b4
    b_far[at["z"]] = b4
    loads[1].wait()
    c4 = jnp.concatenate([c_in[...]] * 4, axis=0).T
    gram_c = gram(c4)[0:32, :] / depth
    loads[2].wait()
    wide = lane_group((depth, 128))
    y = jnp.zeros((128, 128), F32)
    for q in range(4):
        part = x[:, 8 * q : 8 * q + 8, :].reshape(128, depth)
        y = y + dot(part, jnp.where(wide == q, c4, 0.0))
        x_flat[128 * q : 128 * q + 128, :] = part
    y = y.reshape(16, 8, 128)
    y_i[...] = y
    for s in range(8):
        y_j[s] = y[:, s, :]

    pl.semaphore_wait(barrier, len(greeted))

    def go(*args):
        arrive, leave = exchange(*args)
        pending.append(leave)
        return arrive

    b_near_in = go("row", b_send, b_rows)
    b_far_in = go("z", b_send, b_far)
    for step in steps_of("y"):
        pl.semaphore_signal(near, inc=1, device_id=places.device(step), device_id_type=MESH)

    b_near_in.wait()
    b_pack = pack_square(b_rows[...].reshape(32, 128))
    m1 = y_j[0] * b_pack[0:1]
    for s in range(1, 8):
        m1 = m1 + y_j[s] * b_pack[s : s + 1]
    m1 = pack_rows(fold(m1))
    m1_send[...] = m1
    m1_all[at["col"]] = m1
    pl.semaphore_wait(near, len(steps_of("y")))
    m1_in = go("col", m1_send, m1_all)

    b_far_in.wait()
    far = pack_rows(b_far[...].reshape(16, 128))
    g_send[...] = far
    g_all[at["xyc"]] = far
    g_in = go("xyc", g_send, g_all)
    g_in.wait()
    gram_b = quarters_gram(gram(g_all[...].reshape(128, 128))) / total_j
    solve_a = solver(gram_b, gram_c)
    solve_rows = jnp.concatenate([solve_a] * 4, axis=0)
    solve_a = by_quarter(solve_a)

    m1_in.wait()
    m1 = jnp.sum(m1_all[...], axis=0)
    m1 = jnp.concatenate([m1, m1], axis=0)
    a_pack = dot(m1, solve_a)[0:4]
    group8, upper = lane_group((8, 128)), iota((8, 128), 0) // 4
    m1 = jnp.concatenate([jnp.where(group8 == 2 * t + upper, m1, 0.0) for t in range(2)], axis=0)
    a_own = dot(m1, solve_rows)
    a_send[...] = a_pack
    a_all[at["row"]] = a_pack
    a_in = go("row", a_send, a_all)
    a_rows[...] = a_own
    m2 = y_i[0] * a_own[0:1]
    for i in range(1, 16):
        m2 = m2 + y_i[i] * a_own[i : i + 1]
    m2_send[...] = m2
    m2_all[at["x_z"]] = m2
    m2_in = go("x_z", m2_send, m2_all)

    m2_in.wait()
    m2 = jnp.sum(m2_all[...], axis=0)
    m2_half[...] = m2
    m2_pair[at["core"]] = m2
    m2_in = go("core", m2_half, m2_pair)

    a_in.wait()
    gram_h = quarters_gram(gram(a_all[...].reshape(128, 128)))
    a_along, gram_a = scales(gram_h, total_i)
    solve_b = by_quarter(solver(gram_a, gram_c))

    m2_in.wait()
    b_pack = dot((m2_pair[0] + m2_pair[1]) * a_along, solve_b)
    scaled_b = b_pack * a_along
    khatri = (a_own[:, None, :] * scaled_b[None, :, :]).reshape(128, 128).T
    khatri = jnp.concatenate([khatri[32 * q : 32 * q + 32] for q in range(4)], axis=1)
    m3 = dot(khatri, x_flat[...])
    m3_send[...] = m3.reshape(32, 1, 256)
    m3_parts[at["xyc"]] = m3_send[at["xyc"]]
    m3_in = go("xyc", lambda step: m3_send.at[places.index("xyc", step)], m3_parts)
    own = fold(jnp.where(lane_group((8, 128)) == at["row"] // 8, b_pack, 0.0))
    own = jnp.sum(jnp.where(iota((8, 128), 0) == at["row"] % 8, own, 0.0), axis=0, keepdims=True)
    hb_send[...] = own
    hb_far[at["z"]] = own
    hb_far_in = go("z", hb_send, hb_far)
    a_out[...] = (a_rows[pl.ds(at["col"], 1), :] * a_along)[:, 0:RANK]

    m3_in.wait()
    m3 = jnp.sum(m3_parts[...], axis=0)
    m3z_send[...] = m3
    m3_z[at["z"]] = m3
    m3z_in = go("z", m3z_send, m3_z)

    hb_far_in.wait()
    hb = pack_rows(hb_far[...].reshape(16, 128))
    hbx_send[...] = hb
    hb_all[at["xyc"]] = hb
    hb_in = go("xyc", hbx_send, hb_all)

    m3z_in.wait()
    m3 = jnp.sum(m3_z[...], axis=0)
    m3_done_send[...] = m3
    m3_done[at["xyc"]] = m3
    done_in = go("xyc", m3_done_send, m3_done)

    hb_in.wait()
    b_along, gram_b = scales(quarters_gram(gram(hb_all[...].reshape(128, 128))), total_j)
    b_out[...] = (hb_send[...] * b_along)[:, 0:RANK]
    solve_c = (solver(gram_a, gram_b) * b_along)[:, 0:RANK]

    done_in.wait()
    fresh = dot(solve_c, m3_done[...].reshape(RANK, depth))
    norms = jnp.sqrt(jnp.sum(fresh * fresh, axis=1, keepdims=True) / depth + EPS)
    c_out[...] = fresh / norms
    w_out[...] = jnp.sum(norms * eye_rep(), axis=0, keepdims=True)[:, 0:RANK] / 512.0

    for leave in pending:
        leave.wait()


def hand_over(*refs):
    copies = [pltpu.make_async_copy(refs[k], refs[4 + k], refs[8].at[k]) for k in range(4)]
    for copy in copies:
        copy.start()
    for copy in copies:
        copy.wait()


def per_device(tensor, factor_b, initial_third_factor):
    tile = (8, 128)
    vmem = lambda *shape: pltpu.VMEM(shape, F32)
    results = (
        jax.ShapeDtypeStruct((1, RANK), F32),
        jax.ShapeDtypeStruct((1, RANK), F32),
        jax.ShapeDtypeStruct((RANK, 256), F32),
        jax.ShapeDtypeStruct((1, RANK), F32),
    )
    ready = pl.pallas_call(
        kernel,
        out_shape=tuple(pltpu.VMEM(r.shape, F32) for r in results),
        in_specs=[pl.BlockSpec(memory_space=pltpu.HBM)] * 3,
        out_specs=[pl.BlockSpec(memory_space=pltpu.VMEM)] * 4,
        scratch_shapes=[
            vmem(16, 32, 256), vmem(RANK, 256), vmem(1, RANK), vmem(16, *tile), vmem(8, 16, 128), vmem(512, 256),
            vmem(1, 128), vmem(32, 1, 128), vmem(16, 1, 128), vmem(4, 128), vmem(32, 4, 128),
            vmem(4, 128), vmem(16, 4, 128), vmem(4, 128), vmem(32, 4, 128),
            vmem(*tile), vmem(16, *tile), vmem(*tile), vmem(2, *tile),
            vmem(32, 1, 256), vmem(32, 1, 256), vmem(1, 256), vmem(16, 1, 256), vmem(1, 256), vmem(32, 1, 256),
            vmem(1, 128), vmem(16, 1, 128), vmem(4, 128), vmem(32, 4, 128), vmem(16, 128),
            pltpu.SemaphoreType.DMA((3,)), pltpu.SemaphoreType.DMA((12,)), pltpu.SemaphoreType.DMA((12,)),
            pltpu.SemaphoreType.REGULAR,
        ],
        compiler_params=pltpu.CompilerParams(
            collective_id=0, has_side_effects=True, vmem_limit_bytes=40 * 1024 * 1024
        ),
        name="als_sweep",
    )(*[pltpu.with_memory_space_constraint(a, pltpu.HBM) for a in (tensor, factor_b, initial_third_factor.T)])
    a, b, c, w = pl.pallas_call(
        hand_over,
        out_shape=results,
        in_specs=[pl.BlockSpec(memory_space=pltpu.VMEM)] * 4,
        out_specs=[pl.BlockSpec(memory_space=pltpu.HBM)] * 4,
        scratch_shapes=[pltpu.SemaphoreType.DMA((4,))],
        compiler_params=pltpu.CompilerParams(vmem_limit_bytes=1024 * 1024),
        name="hand_over",
    )(*ready)
    return a, b, c.T, w.reshape(RANK)


def solution(mesh):
    return jax.shard_map(
        per_device,
        mesh=mesh,
        in_specs=(P("row", "col", None), P(("col", "row"), None), P()),
        out_specs=(P(("row", "col"), None), P(("col", "row"), None), P(), P()),
        check_vma=False,
    )
```

```python
import functools
import itertools

import jax
import jax.numpy as jnp
from jax import lax
from jax.experimental import pallas as pl
from jax.experimental.pallas import tpu as pltpu
from jax.sharding import PartitionSpec as P

HI = lax.Precision.HIGHEST
EPS = 1e-05
RIDGE_PENALTY = 0.05
MESH = pl.DeviceIdType.MESH
F32 = jnp.float32
RANK = 32
SIZES = {"x": 4, "z_lo": 4, "core": 2, "z_hi": 4, "y": 4}
GROUPS = {
    "row": ("x", "z_lo", "core"),
    "z": ("z_hi", "z_lo"),
    "xyc": ("x", "y", "core"),
    "col": ("z_hi", "y"),
    "x_z": ("x", "z_lo"),
    "core": ("core",),
    "y": ("y",),
}


def iota(shape, dim):
    return lax.broadcasted_iota(jnp.int32, shape, dim)


def dot(a, b):
    return lax.dot_general(a, b, (((1,), (0,)), ((), ())), precision=HI, preferred_element_type=F32)


def gram(a):
    return lax.dot_general(a, a, (((0,), (0,)), ((), ())), precision=HI, preferred_element_type=F32)


def roll(a, by):
    return pltpu.roll(a, by, a.ndim - 1)


class Places:
    def __init__(self):
        row, col = lax.axis_index("row"), lax.axis_index("col")
        rem, div = lax.rem, lax.div
        self.own = {"x": div(row, 8), "z_lo": rem(div(row, 2), 4), "core": rem(row, 2), "z_hi": div(col, 4), "y": rem(col, 4)}
        self.weight = {"x": 8, "z_lo": 2, "core": 1, "z_hi": 4, "y": 1}
        self.known = {}

    def coordinate(self, dim, step):
        if (dim, step) not in self.known:
            there = lax.rem(self.own[dim] + step, SIZES[dim]) if step else self.own[dim]
            self.known[dim, step] = there, there * self.weight[dim]
        return self.known[dim, step]

    def device(self, step, core=None):
        at = {d: self.coordinate(d, step.get(d, 0))[1] for d in SIZES}
        if core is not None:
            at["core"] = core
        return {"row": at["x"] + at["z_lo"] + at["core"], "col": at["z_hi"] + at["y"]}

    def index(self, group, step=None):
        index = 0
        for d in GROUPS[group]:
            index = index * SIZES[d] + self.coordinate(d, (step or {}).get(d, 0))[0]
        return index


def steps_of(group):
    dims = GROUPS[group]
    steps = [s for s in itertools.product(*[range(SIZES[d]) for d in dims]) if any(s)]
    return farthest_first([{d: n for d, n in zip(dims, s) if n} for s in steps])


def farthest_first(steps):
    far = {"x": 1, "y": 1, "z_lo": 1, "core": 0, "z_hi": 4}
    return sorted(steps, key=lambda step: sum(far[d] * min(n, SIZES[d] - n) for d, n in step.items()), reverse=True)


def lane_group(shape):
    return iota(shape, len(shape) - 1) // RANK


def eye_rep():
    return jnp.where(iota((RANK, 128), 0) == iota((RANK, 128), 1) % RANK, 1.0, 0.0).astype(F32)


def fold(a):
    a = a + roll(a, 64)
    return a + roll(a, 32)


def quarters_gram(h):
    g = lane_group((RANK, 128))
    t = jnp.where(g == 0, h[0:32, :], jnp.where(g == 1, h[32:64, :], jnp.where(g == 2, h[64:96, :], h[96:128, :])))
    return fold(t)


def pack_square(m):
    g = lane_group((8, 128))
    return jnp.where(g == 0, m[0:8], jnp.where(g == 1, m[8:16], jnp.where(g == 2, m[16:24], m[24:32])))


def pack_rows(m):
    g = lane_group((8, 128))
    low, high = (jnp.where(g % 2 == 1, pltpu.roll(half, 4, 0), half) for half in (m[0:8], m[8:16]))
    return jnp.where(g < 2, low, high)[0:4]


def by_quarter(m):
    g = lane_group((RANK, 128))
    return jnp.concatenate([jnp.where(g == q, m, 0.0) for q in range(4)], axis=0)


def inverse(s):
    width, block = 128, 8
    rows, lanes = iota((RANK, width), 0), iota((RANK, width), 1)
    a = jnp.where(lanes < RANK, s, eye_rep())
    for k in range(0, RANK, block):
        c = [jnp.broadcast_to(a[:, k + j : k + j + 1], (RANK, width)) for j in range(block)]
        r = [a[k + j : k + j + 1, :] for j in range(block)]
        p = [[c[j][k + i : k + i + 1, :] for j in range(block)] for i in range(block)]
        for i in range(block):
            ip = 1.0 / p[i][i]
            r[i] = r[i] * ip
            for j in range(i + 1, block):
                p[i][j] = p[i][j] * ip
            for other in range(block):
                if other != i:
                    f = p[other][i]
                    r[other] = r[other] - f * r[i]
                    for j in range(i + 1, block):
                        p[other][j] = p[other][j] - f * p[i][j]
        u = c[0] * r[0]
        for j in range(1, block):
            u = u + c[j] * r[j]
        new = a - u
        pieces = [new[i : i + block] for i in range(0, RANK, block)]
        pieces[k // block] = jnp.concatenate(r, axis=0)
        a = jnp.concatenate(pieces, axis=0)
    return jnp.where(lanes < RANK, roll(a, 32), a)


def solver(gram_u, gram_w):
    eye = eye_rep()
    v = gram_u * gram_w
    trace = jnp.sum(jnp.sum(v * eye, axis=0, keepdims=True), axis=1, keepdims=True) / 4.0
    return inverse(v + (RIDGE_PENALTY / RANK) * trace * eye)


def scales(h, count):
    masked = h * eye_rep()
    along = 1.0 / jnp.sqrt(jnp.sum(masked, axis=0, keepdims=True) / count + EPS)
    down = 1.0 / jnp.sqrt(jnp.sum(masked, axis=1, keepdims=True) / 4.0 / count + EPS)
    return along, h * along * down / count


def kernel(tensor_hbm, b_hbm, c_hbm, a_out, b_out, c_out, w_out,
           x, c_in, b_in, y_i, y_j, x_flat, b_send, b_rows, b_far, g_send, g_all,
           m1_send, m1_all, a_send, a_all, m2_send, m2_all, m2_half, m2_pair, m3_send, m3_parts, m3z_send, m3_z, m3_done_send, m3_done,
           hb_send, hb_far, hbx_send, hb_all, a_rows, local, sent, got, known):
    places = Places()
    at = {g: places.index(g) for g in GROUPS}
    total_i, total_j, depth = 512, 512, 256

    barrier = pltpu.get_barrier_semaphore()
    near_known, line_known, lines_known, all_known = (known.at[k] for k in range(4))
    on_core = [places.own["core"] == 0, places.own["core"] == 1]
    partner = places.device({"core": 1})

    def tell(semaphore, target):
        pl.semaphore_signal(semaphore, inc=1, device_id=target, device_id_type=MESH)

    @pl.when(on_core[0])
    def _():
        tell(barrier, partner)

    for step in steps_of("x_z") + steps_of("y"):
        tell(barrier, places.device(step, core=1))
    for step in steps_of("z"):
        tell(barrier, places.device(step, core=0))

    loads = [
        pltpu.make_async_copy(b_hbm, b_in, local.at[0]),
        pltpu.make_async_copy(c_hbm, c_in, local.at[1]),
        pltpu.make_async_copy(tensor_hbm, x, local.at[2]),
    ]
    for load in loads:
        load.start()

    rounds = itertools.count()
    pending = []

    def exchange(group, source, buffer):
        k = next(rounds)
        steps = steps_of(group)
        for step in steps:
            src = source(step) if callable(source) else source
            pltpu.make_async_remote_copy(
                src_ref=src, dst_ref=buffer.at[at[group]], send_sem=sent.at[k], recv_sem=got.at[k],
                device_id=places.device(step), device_id_type=MESH,
            ).start()
        n = len(steps)
        span = buffer.at[pl.ds(0, n)]
        return pltpu.make_async_copy(span, span, got.at[k]), pltpu.make_async_copy(span, span, sent.at[k])

    loads[0].wait()
    b4 = jnp.concatenate([b_in[...]] * 4, axis=1)
    b_send[...] = b4
    b_rows[at["row"]] = b4
    b_far[at["z"]] = b4
    loads[1].wait()
    c4 = jnp.concatenate([c_in[...]] * 4, axis=0).T
    gram_c = gram(c4)[0:32, :] / depth
    loads[2].wait()
    wide = lane_group((depth, 128))
    y = jnp.zeros((128, 128), F32)
    for q in range(4):
        part = x[:, 8 * q : 8 * q + 8, :].reshape(128, depth)
        y = y + dot(part, jnp.where(wide == q, c4, 0.0))
        x_flat[128 * q : 128 * q + 128, :] = part
    y = y.reshape(16, 8, 128)
    y_i[...] = y
    for s in range(8):
        y_j[s] = y[:, s, :]

    @pl.when(on_core[1])
    def _():
        pl.semaphore_wait(barrier, len(steps_of("row")) + 2 * len(steps_of("y")))
        tell(near_known, partner)

    @pl.when(on_core[0])
    def _():
        pl.semaphore_wait(near_known, 1)

    def go(*args):
        arrive, leave = exchange(*args)
        pending.append(leave)
        return arrive

    b_near_in = go("row", b_send, b_rows)

    @pl.when(on_core[0])
    def _():
        pl.semaphore_wait(barrier, 2 * len(steps_of("z")))
        tell(line_known, partner)
        for step in steps_of("y"):
            tell(lines_known, places.device(step))

    @pl.when(on_core[1])
    def _():
        pl.semaphore_wait(line_known, 1)

    b_far_in = go("z", b_send, b_far)

    b_near_in.wait()
    b_pack = pack_square(b_rows[...].reshape(32, 128))
    m1 = y_j[0] * b_pack[0:1]
    for s in range(1, 8):
        m1 = m1 + y_j[s] * b_pack[s : s + 1]
    m1 = pack_rows(fold(m1))
    m1_send[...] = m1
    m1_all[at["col"]] = m1

    @pl.when(on_core[0])
    def _():
        pl.semaphore_wait(lines_known, len(steps_of("y")))
        tell(all_known, partner)

    @pl.when(on_core[1])
    def _():
        pl.semaphore_wait(all_known, 1)

    m1_in = go("col", m1_send, m1_all)

    b_far_in.wait()
    far = pack_rows(b_far[...].reshape(16, 128))
    g_send[...] = far
    g_all[at["xyc"]] = far
    g_in = go("xyc", g_send, g_all)
    m1_in.wait()
    m1 = jnp.sum(m1_all[...], axis=0)
    a_send[...] = m1
    a_all[at["row"]] = m1
    a_in = go("row", a_send, a_all)

    g_in.wait()
    gram_b = quarters_gram(gram(g_all[...].reshape(128, 128))) / total_j
    solve_a = solver(gram_b, gram_c)
    m1 = jnp.concatenate([m1, m1], axis=0)
    group8, upper = lane_group((8, 128)), iota((8, 128), 0) // 4
    m1 = jnp.concatenate([jnp.where(group8 == 2 * t + upper, m1, 0.0) for t in range(2)], axis=0)
    a_own = dot(m1, jnp.concatenate([solve_a] * 4, axis=0))
    m2 = y_i[0] * a_own[0:1]
    for i in range(1, 16):
        m2 = m2 + y_i[i] * a_own[i : i + 1]
    m2_send[...] = m2
    m2_all[at["x_z"]] = m2
    m2_in = go("x_z", m2_send, m2_all)
    a_rows[...] = a_own

    a_in.wait()
    a_every = dot(a_all[...].reshape(128, 128), by_quarter(solve_a))
    a_along, gram_a = scales(quarters_gram(gram(a_every)), total_i)

    solve_b = by_quarter(solver(gram_a, gram_c))
    m2_in.wait()
    m2 = jnp.sum(m2_all[...], axis=0)
    m2_half[...] = m2
    m2_pair[at["core"]] = m2
    m2_in = go("core", m2_half, m2_pair)

    m2_in.wait()
    b_pack = dot((m2_pair[0] + m2_pair[1]) * a_along, solve_b)
    scaled_b = b_pack * a_along
    khatri = (a_own[:, None, :] * scaled_b[None, :, :]).reshape(128, 128).T
    khatri = jnp.concatenate([khatri[32 * q : 32 * q + 32] for q in range(4)], axis=1)
    m3 = dot(khatri, x_flat[...])
    m3_send[...] = m3.reshape(32, 1, 256)
    m3_parts[at["xyc"]] = m3_send[at["xyc"]]
    m3_in = go("xyc", lambda step: m3_send.at[places.index("xyc", step)], m3_parts)
    own = fold(jnp.where(lane_group((8, 128)) == at["row"] // 8, b_pack, 0.0))
    own = jnp.sum(jnp.where(iota((8, 128), 0) == at["row"] % 8, own, 0.0), axis=0, keepdims=True)
    hb_send[...] = own
    hb_far[at["z"]] = own
    hb_far_in = go("z", hb_send, hb_far)
    a_out[...] = (a_rows[pl.ds(at["col"], 1), :] * a_along)[:, 0:RANK]

    m3_in.wait()
    m3 = jnp.sum(m3_parts[...], axis=0)
    m3z_send[...] = m3
    m3_z[at["z"]] = m3
    m3z_in = go("z", m3z_send, m3_z)

    hb_far_in.wait()
    hb = pack_rows(hb_far[...].reshape(16, 128))
    hbx_send[...] = hb
    hb_all[at["xyc"]] = hb
    hb_in = go("xyc", hbx_send, hb_all)

    m3z_in.wait()
    m3 = jnp.sum(m3_z[...], axis=0)
    m3_done_send[...] = m3
    m3_done[at["xyc"]] = m3
    done_in = go("xyc", m3_done_send, m3_done)

    hb_in.wait()
    b_along, gram_b = scales(quarters_gram(gram(hb_all[...].reshape(128, 128))), total_j)
    b_out[...] = (hb_send[...] * b_along)[:, 0:RANK]
    solve_c = (solver(gram_a, gram_b) * b_along)[:, 0:RANK]

    done_in.wait()
    fresh = dot(solve_c, m3_done[...].reshape(RANK, depth))
    norms = jnp.sqrt(jnp.sum(fresh * fresh, axis=1, keepdims=True) / depth + EPS)
    c_out[...] = fresh / norms
    w_out[...] = jnp.sum(norms * eye_rep(), axis=0, keepdims=True)[:, 0:RANK] / 512.0

    for leave in pending:
        leave.wait()


def hand_over(*refs):
    copies = [pltpu.make_async_copy(refs[k], refs[4 + k], refs[8].at[k]) for k in range(4)]
    for copy in copies:
        copy.start()
    for copy in copies:
        copy.wait()


def per_device(tensor, factor_b, initial_third_factor):
    tile = (8, 128)
    vmem = lambda *shape: pltpu.VMEM(shape, F32)
    results = (
        jax.ShapeDtypeStruct((1, RANK), F32),
        jax.ShapeDtypeStruct((1, RANK), F32),
        jax.ShapeDtypeStruct((RANK, 256), F32),
        jax.ShapeDtypeStruct((1, RANK), F32),
    )
    ready = pl.pallas_call(
        kernel,
        out_shape=tuple(pltpu.VMEM(r.shape, F32) for r in results),
        in_specs=[pl.BlockSpec(memory_space=pltpu.HBM)] * 3,
        out_specs=[pl.BlockSpec(memory_space=pltpu.VMEM)] * 4,
        scratch_shapes=[
            vmem(16, 32, 256), vmem(RANK, 256), vmem(1, RANK), vmem(16, *tile), vmem(8, 16, 128), vmem(512, 256),
            vmem(1, 128), vmem(32, 1, 128), vmem(16, 1, 128), vmem(4, 128), vmem(32, 4, 128),
            vmem(4, 128), vmem(16, 4, 128), vmem(4, 128), vmem(32, 4, 128),
            vmem(*tile), vmem(16, *tile), vmem(*tile), vmem(2, *tile),
            vmem(32, 1, 256), vmem(32, 1, 256), vmem(1, 256), vmem(16, 1, 256), vmem(1, 256), vmem(32, 1, 256),
            vmem(1, 128), vmem(16, 1, 128), vmem(4, 128), vmem(32, 4, 128), vmem(16, 128),
            pltpu.SemaphoreType.DMA((3,)), pltpu.SemaphoreType.DMA((12,)), pltpu.SemaphoreType.DMA((12,)),
            pltpu.SemaphoreType.REGULAR((4,)),
        ],
        compiler_params=pltpu.CompilerParams(
            collective_id=0, has_side_effects=True, vmem_limit_bytes=40 * 1024 * 1024
        ),
        name="als_sweep",
    )(*[pltpu.with_memory_space_constraint(a, pltpu.HBM) for a in (tensor, factor_b, initial_third_factor.T)])
    a, b, c, w = pl.pallas_call(
        hand_over,
        out_shape=results,
        in_specs=[pl.BlockSpec(memory_space=pltpu.VMEM)] * 4,
        out_specs=[pl.BlockSpec(memory_space=pltpu.HBM)] * 4,
        scratch_shapes=[pltpu.SemaphoreType.DMA((4,))],
        compiler_params=pltpu.CompilerParams(vmem_limit_bytes=1024 * 1024),
        name="hand_over",
    )(*ready)
    return a, b, c.T, w.reshape(RANK)


def solution(mesh):
    return jax.shard_map(
        per_device,
        mesh=mesh,
        in_specs=(P("row", "col", None), P(("col", "row"), None), P()),
        out_specs=(P(("row", "col"), None), P(("col", "row"), None), P(), P()),
        check_vma=False,
    )
```

```python
import functools
import itertools

import jax
import jax.numpy as jnp
from jax import lax
from jax.experimental import pallas as pl
from jax.experimental.pallas import tpu as pltpu
from jax.sharding import PartitionSpec as P

HI = lax.Precision.HIGHEST
EPS = 1e-05
RIDGE_PENALTY = 0.05
MESH = pl.DeviceIdType.MESH
F32 = jnp.float32
RANK = 32
SIZES = {"x": 4, "z_lo": 4, "core": 2, "z_hi": 4, "y": 4}
GROUPS = {
    "row": ("x", "z_lo", "core"),
    "z": ("z_hi", "z_lo"),
    "xyc": ("x", "y", "core"),
    "col": ("z_hi", "y"),
    "x_z": ("x", "z_lo"),
    "core": ("core",),
    "y": ("y",),
}


def iota(shape, dim):
    return lax.broadcasted_iota(jnp.int32, shape, dim)


def dot(a, b):
    return lax.dot_general(a, b, (((1,), (0,)), ((), ())), precision=HI, preferred_element_type=F32)


def gram(a):
    return lax.dot_general(a, a, (((0,), (0,)), ((), ())), precision=HI, preferred_element_type=F32)


def roll(a, by):
    return pltpu.roll(a, by, a.ndim - 1)


class Places:
    def __init__(self):
        row, col = lax.axis_index("row"), lax.axis_index("col")
        rem, div = lax.rem, lax.div
        self.own = {"x": div(row, 8), "z_lo": rem(div(row, 2), 4), "core": rem(row, 2), "z_hi": div(col, 4), "y": rem(col, 4)}
        self.weight = {"x": 8, "z_lo": 2, "core": 1, "z_hi": 4, "y": 1}
        self.known = {}

    def coordinate(self, dim, step):
        if (dim, step) not in self.known:
            there = lax.rem(self.own[dim] + step, SIZES[dim]) if step else self.own[dim]
            self.known[dim, step] = there, there * self.weight[dim]
        return self.known[dim, step]

    def device(self, step, core=None):
        at = {d: self.coordinate(d, step.get(d, 0))[1] for d in SIZES}
        if core is not None:
            at["core"] = core
        return {"row": at["x"] + at["z_lo"] + at["core"], "col": at["z_hi"] + at["y"]}

    def index(self, group, step=None):
        index = 0
        for d in GROUPS[group]:
            index = index * SIZES[d] + self.coordinate(d, (step or {}).get(d, 0))[0]
        return index


def steps_of(group):
    dims = GROUPS[group]
    steps = [s for s in itertools.product(*[range(SIZES[d]) for d in dims]) if any(s)]
    return farthest_first([{d: n for d, n in zip(dims, s) if n} for s in steps])


def farthest_first(steps):
    far = {"x": 1, "y": 1, "z_lo": 1, "core": 0, "z_hi": 4}
    return sorted(steps, key=lambda step: sum(far[d] * min(n, SIZES[d] - n) for d, n in step.items()), reverse=True)


def lane_group(shape):
    return iota(shape, len(shape) - 1) // RANK


def eye_rep():
    return jnp.where(iota((RANK, 128), 0) == iota((RANK, 128), 1) % RANK, 1.0, 0.0).astype(F32)


def fold(a):
    a = a + roll(a, 64)
    return a + roll(a, 32)


def quarters_gram(h):
    g = lane_group((RANK, 128))
    t = jnp.where(g == 0, h[0:32, :], jnp.where(g == 1, h[32:64, :], jnp.where(g == 2, h[64:96, :], h[96:128, :])))
    return fold(t)


def pack_square(m):
    g = lane_group((8, 128))
    return jnp.where(g == 0, m[0:8], jnp.where(g == 1, m[8:16], jnp.where(g == 2, m[16:24], m[24:32])))


def pack_rows(m):
    g = lane_group((8, 128))
    low, high = (jnp.where(g % 2 == 1, pltpu.roll(half, 4, 0), half) for half in (m[0:8], m[8:16]))
    return jnp.where(g < 2, low, high)[0:4]


def by_quarter(m):
    g = lane_group((RANK, 128))
    return jnp.concatenate([jnp.where(g == q, m, 0.0) for q in range(4)], axis=0)


def inverse(s):
    width, block = 128, 16
    lanes, row = iota((RANK, width), 1), iota((block, width), 0)
    a = jnp.where(lanes < RANK, s, eye_rep())
    for k in range(0, RANK, block):
        columns = [jnp.broadcast_to(a[:, k + j : k + j + 1], (RANK, width)) for j in range(block)]
        rows = a[k : k + block]
        p = [column[k : k + block] for column in columns]
        for i in range(block):
            pivot = 1.0 / p[i][i : i + 1]
            here = row == i
            factor = jnp.where(here, 0.0, p[i])
            own = rows[i : i + 1] * pivot
            rows = jnp.where(here, own, rows) - factor * own
            for j in range(i + 1, block):
                own = p[j][i : i + 1] * pivot
                p[j] = jnp.where(here, own, p[j]) - factor * own
        u = columns[0] * rows[0:1]
        for j in range(1, block):
            u = u + columns[j] * rows[j : j + 1]
        pieces = [(a - u)[i : i + block] for i in range(0, RANK, block)]
        pieces[k // block] = rows
        a = jnp.concatenate(pieces, axis=0)
    return jnp.where(lanes < RANK, roll(a, 32), a)


def solver(gram_u, gram_w):
    eye = eye_rep()
    v = gram_u * gram_w
    trace = jnp.sum(jnp.sum(v * eye, axis=0, keepdims=True), axis=1, keepdims=True) / 4.0
    return inverse(v + (RIDGE_PENALTY / RANK) * trace * eye)


def scales(h, count):
    masked = h * eye_rep()
    along = 1.0 / jnp.sqrt(jnp.sum(masked, axis=0, keepdims=True) / count + EPS)
    down = 1.0 / jnp.sqrt(jnp.sum(masked, axis=1, keepdims=True) / 4.0 / count + EPS)
    return along, h * along * down / count


def kernel(tensor_hbm, b_hbm, c_hbm, a_out, b_out, c_out, w_out,
           x, c_in, b_in, y_i, y_j, x_flat, b_send, b_rows, b_far, g_send, g_all,
           m1_send, m1_all, a_send, a_all, m2_send, m2_all, m2_half, m2_pair, m3_send, m3_parts, m3z_send, m3_z, m3_done_send, m3_done,
           hb_send, hb_far, hbx_send, hb_all, a_rows, local, sent, got, known):
    places = Places()
    at = {g: places.index(g) for g in GROUPS}
    total_i, total_j, depth = 512, 512, 256

    barrier = pltpu.get_barrier_semaphore()
    near_known, line_known, lines_known, all_known = (known.at[k] for k in range(4))
    on_core = [places.own["core"] == 0, places.own["core"] == 1]
    partner = places.device({"core": 1})

    def tell(semaphore, target):
        pl.semaphore_signal(semaphore, inc=1, device_id=target, device_id_type=MESH)

    @pl.when(on_core[0])
    def _():
        tell(barrier, partner)

    for step in steps_of("z"):
        tell(barrier, places.device(step, core=0))
    for step in steps_of("x_z") + steps_of("y"):
        tell(barrier, places.device(step, core=1))

    loads = [
        pltpu.make_async_copy(b_hbm, b_in, local.at[0]),
        pltpu.make_async_copy(c_hbm, c_in, local.at[1]),
        pltpu.make_async_copy(tensor_hbm, x, local.at[2]),
    ]
    for load in loads:
        load.start()

    rounds = itertools.count()
    pending = []

    def exchange(group, source, buffer):
        k = next(rounds)
        steps = steps_of(group)
        for step in steps:
            src = source(step) if callable(source) else source
            pltpu.make_async_remote_copy(
                src_ref=src, dst_ref=buffer.at[at[group]], send_sem=sent.at[k], recv_sem=got.at[k],
                device_id=places.device(step), device_id_type=MESH,
            ).start()
        n = len(steps)
        span = buffer.at[pl.ds(0, n)]
        return pltpu.make_async_copy(span, span, got.at[k]), pltpu.make_async_copy(span, span, sent.at[k])

    loads[0].wait()
    b4 = jnp.concatenate([b_in[...]] * 4, axis=1)
    b_send[...] = b4
    b_rows[at["row"]] = b4
    b_far[at["z"]] = b4
    loads[1].wait()
    c4 = jnp.concatenate([c_in[...]] * 4, axis=0).T
    gram_c = gram(c4)[0:32, :] / depth
    loads[2].wait()
    wide = lane_group((depth, 128))
    y = jnp.zeros((128, 128), F32)
    for q in range(4):
        part = x[:, 8 * q : 8 * q + 8, :].reshape(128, depth)
        y = y + dot(part, jnp.where(wide == q, c4, 0.0))
        x_flat[128 * q : 128 * q + 128, :] = part
    y = y.reshape(16, 8, 128)
    y_i[...] = y
    for s in range(8):
        y_j[s] = y[:, s, :]

    @pl.when(on_core[1])
    def _():
        pl.semaphore_wait(barrier, len(steps_of("row")) + 2 * len(steps_of("y")))
        tell(near_known, partner)

    @pl.when(on_core[0])
    def _():
        pl.semaphore_wait(near_known, 1)

    def go(*args):
        arrive, leave = exchange(*args)
        pending.append(leave)
        return arrive

    b_near_in = go("row", b_send, b_rows)

    @pl.when(on_core[0])
    def _():
        pl.semaphore_wait(barrier, 2 * len(steps_of("z")))
        tell(line_known, partner)
        for step in steps_of("y"):
            tell(lines_known, places.device(step))

    @pl.when(on_core[1])
    def _():
        pl.semaphore_wait(line_known, 1)

    b_far_in = go("z", b_send, b_far)

    b_near_in.wait()
    b_pack = pack_square(b_rows[...].reshape(32, 128))
    m1 = y_j[0] * b_pack[0:1]
    for s in range(1, 8):
        m1 = m1 + y_j[s] * b_pack[s : s + 1]
    m1 = pack_rows(fold(m1))
    m1_send[...] = m1
    m1_all[at["col"]] = m1

    @pl.when(on_core[0])
    def _():
        pl.semaphore_wait(lines_known, len(steps_of("y")))
        tell(all_known, partner)

    @pl.when(on_core[1])
    def _():
        pl.semaphore_wait(all_known, 1)

    m1_in = go("col", m1_send, m1_all)

    b_far_in.wait()
    far = pack_rows(b_far[...].reshape(16, 128))
    g_send[...] = far
    g_all[at["xyc"]] = far
    g_in = go("xyc", g_send, g_all)
    m1_in.wait()
    m1 = jnp.sum(m1_all[...], axis=0)
    a_send[...] = m1
    a_all[at["row"]] = m1
    a_in = go("row", a_send, a_all)

    g_in.wait()
    gram_b = quarters_gram(gram(g_all[...].reshape(128, 128))) / total_j
    solve_a = solver(gram_b, gram_c)
    m1 = jnp.concatenate([m1, m1], axis=0)
    group8, upper = lane_group((8, 128)), iota((8, 128), 0) // 4
    m1 = jnp.concatenate([jnp.where(group8 == 2 * t + upper, m1, 0.0) for t in range(2)], axis=0)
    a_own = dot(m1, jnp.concatenate([solve_a] * 4, axis=0))
    m2 = y_i[0] * a_own[0:1]
    for i in range(1, 16):
        m2 = m2 + y_i[i] * a_own[i : i + 1]
    m2_send[...] = m2
    m2_all[at["x_z"]] = m2
    m2_in = go("x_z", m2_send, m2_all)
    a_rows[...] = a_own

    a_in.wait()
    a_every = dot(a_all[...].reshape(128, 128), by_quarter(solve_a))
    a_along, gram_a = scales(quarters_gram(gram(a_every)), total_i)

    solve_b = by_quarter(solver(gram_a, gram_c))
    m2_in.wait()
    m2 = jnp.sum(m2_all[...], axis=0)
    m2_half[...] = m2
    m2_pair[at["core"]] = m2
    m2_in = go("core", m2_half, m2_pair)

    m2_in.wait()
    b_pack = dot((m2_pair[0] + m2_pair[1]) * a_along, solve_b)
    scaled_b = b_pack * a_along
    khatri = (a_own[:, None, :] * scaled_b[None, :, :]).reshape(128, 128).T
    khatri = jnp.concatenate([khatri[32 * q : 32 * q + 32] for q in range(4)], axis=1)
    m3 = dot(khatri, x_flat[...])
    m3_send[...] = m3.reshape(32, 1, 256)
    m3_parts[at["xyc"]] = m3_send[at["xyc"]]
    m3_in = go("xyc", lambda step: m3_send.at[places.index("xyc", step)], m3_parts)
    own = fold(jnp.where(lane_group((8, 128)) == at["row"] // 8, b_pack, 0.0))
    own = jnp.sum(jnp.where(iota((8, 128), 0) == at["row"] % 8, own, 0.0), axis=0, keepdims=True)
    hb_send[...] = own
    hb_far[at["z"]] = own
    hb_far_in = go("z", hb_send, hb_far)
    a_out[...] = (a_rows[pl.ds(at["col"], 1), :] * a_along)[:, 0:RANK]

    m3_in.wait()
    m3 = jnp.sum(m3_parts[...], axis=0)
    m3z_send[...] = m3
    m3_z[at["z"]] = m3
    m3z_in = go("z", m3z_send, m3_z)

    hb_far_in.wait()
    hb = pack_rows(hb_far[...].reshape(16, 128))
    hbx_send[...] = hb
    hb_all[at["xyc"]] = hb
    hb_in = go("xyc", hbx_send, hb_all)

    m3z_in.wait()
    m3 = jnp.sum(m3_z[...], axis=0)
    m3_done_send[...] = m3
    m3_done[at["xyc"]] = m3
    done_in = go("xyc", m3_done_send, m3_done)

    hb_in.wait()
    b_along, gram_b = scales(quarters_gram(gram(hb_all[...].reshape(128, 128))), total_j)
    b_out[...] = (hb_send[...] * b_along)[:, 0:RANK]
    solve_c = (solver(gram_a, gram_b) * b_along)[:, 0:RANK]

    done_in.wait()
    fresh = dot(solve_c, m3_done[...].reshape(RANK, depth))
    norms = jnp.sqrt(jnp.sum(fresh * fresh, axis=1, keepdims=True) / depth + EPS)
    c_out[...] = fresh / norms
    w_out[...] = jnp.sum(norms * eye_rep(), axis=0, keepdims=True)[:, 0:RANK] / 512.0

    for leave in pending:
        leave.wait()


def hand_over(*refs):
    copies = [pltpu.make_async_copy(refs[k], refs[4 + k], refs[8].at[k]) for k in range(4)]
    for copy in copies:
        copy.start()
    for copy in copies:
        copy.wait()


def per_device(tensor, factor_b, initial_third_factor):
    tile = (8, 128)
    vmem = lambda *shape: pltpu.VMEM(shape, F32)
    results = (
        jax.ShapeDtypeStruct((1, RANK), F32),
        jax.ShapeDtypeStruct((1, RANK), F32),
        jax.ShapeDtypeStruct((RANK, 256), F32),
        jax.ShapeDtypeStruct((1, RANK), F32),
    )
    ready = pl.pallas_call(
        kernel,
        out_shape=tuple(pltpu.VMEM(r.shape, F32) for r in results),
        in_specs=[pl.BlockSpec(memory_space=pltpu.HBM)] * 3,
        out_specs=[pl.BlockSpec(memory_space=pltpu.VMEM)] * 4,
        scratch_shapes=[
            vmem(16, 32, 256), vmem(RANK, 256), vmem(1, RANK), vmem(16, *tile), vmem(8, 16, 128), vmem(512, 256),
            vmem(1, 128), vmem(32, 1, 128), vmem(16, 1, 128), vmem(4, 128), vmem(32, 4, 128),
            vmem(4, 128), vmem(16, 4, 128), vmem(4, 128), vmem(32, 4, 128),
            vmem(*tile), vmem(16, *tile), vmem(*tile), vmem(2, *tile),
            vmem(32, 1, 256), vmem(32, 1, 256), vmem(1, 256), vmem(16, 1, 256), vmem(1, 256), vmem(32, 1, 256),
            vmem(1, 128), vmem(16, 1, 128), vmem(4, 128), vmem(32, 4, 128), vmem(16, 128),
            pltpu.SemaphoreType.DMA((3,)), pltpu.SemaphoreType.DMA((12,)), pltpu.SemaphoreType.DMA((12,)),
            pltpu.SemaphoreType.REGULAR((4,)),
        ],
        compiler_params=pltpu.CompilerParams(
            collective_id=0, has_side_effects=True, vmem_limit_bytes=40 * 1024 * 1024
        ),
        name="als_sweep",
    )(*[pltpu.with_memory_space_constraint(a, pltpu.HBM) for a in (tensor, factor_b, initial_third_factor.T)])
    a, b, c, w = pl.pallas_call(
        hand_over,
        out_shape=results,
        in_specs=[pl.BlockSpec(memory_space=pltpu.VMEM)] * 4,
        out_specs=[pl.BlockSpec(memory_space=pltpu.HBM)] * 4,
        scratch_shapes=[pltpu.SemaphoreType.DMA((4,))],
        compiler_params=pltpu.CompilerParams(vmem_limit_bytes=1024 * 1024),
        name="hand_over",
    )(*ready)
    return a, b, c.T, w.reshape(RANK)


def solution(mesh):
    return jax.shard_map(
        per_device,
        mesh=mesh,
        in_specs=(P("row", "col", None), P(("col", "row"), None), P()),
        out_specs=(P(("row", "col"), None), P(("col", "row"), None), P(), P()),
        check_vma=False,
    )
```

```python
import functools
import itertools

import jax
import jax.numpy as jnp
from jax import lax
from jax.experimental import pallas as pl
from jax.experimental.pallas import tpu as pltpu
from jax.sharding import PartitionSpec as P

HI = lax.Precision.HIGHEST
EPS = 1e-05
RIDGE_PENALTY = 0.05
MESH = pl.DeviceIdType.MESH
F32 = jnp.float32
RANK = 32
SIZES = {"x": 4, "z_lo": 4, "core": 2, "z_hi": 4, "y": 4}
GROUPS = {
    "row": ("x", "z_lo", "core"),
    "z": ("z_hi", "z_lo"),
    "xyc": ("x", "y", "core"),
    "col": ("z_hi", "y"),
    "x_z": ("x", "z_lo"),
    "core": ("core",),
    "y": ("y",),
}


def iota(shape, dim):
    return lax.broadcasted_iota(jnp.int32, shape, dim)


def dot(a, b):
    return lax.dot_general(a, b, (((1,), (0,)), ((), ())), precision=HI, preferred_element_type=F32)


def plain_dot(a, b):
    return lax.dot_general(a, b, (((1,), (0,)), ((), ())), preferred_element_type=F32)


def split(a):
    high = a.astype(jnp.bfloat16)
    rest = a - high.astype(F32)
    middle = rest.astype(jnp.bfloat16)
    return high, middle, (rest - middle.astype(F32)).astype(jnp.bfloat16)


def gram(a):
    return lax.dot_general(a, a, (((0,), (0,)), ((), ())), precision=HI, preferred_element_type=F32)


def roll(a, by):
    return pltpu.roll(a, by, a.ndim - 1)


class Places:
    def __init__(self):
        row, col = lax.axis_index("row"), lax.axis_index("col")
        rem, div = lax.rem, lax.div
        self.own = {"x": div(row, 8), "z_lo": rem(div(row, 2), 4), "core": rem(row, 2), "z_hi": div(col, 4), "y": rem(col, 4)}
        self.weight = {"x": 8, "z_lo": 2, "core": 1, "z_hi": 4, "y": 1}
        self.known = {}

    def coordinate(self, dim, step):
        if (dim, step) not in self.known:
            there = lax.rem(self.own[dim] + step, SIZES[dim]) if step else self.own[dim]
            self.known[dim, step] = there, there * self.weight[dim]
        return self.known[dim, step]

    def device(self, step, core=None):
        at = {d: self.coordinate(d, step.get(d, 0))[1] for d in SIZES}
        if core is not None:
            at["core"] = core
        return {"row": at["x"] + at["z_lo"] + at["core"], "col": at["z_hi"] + at["y"]}

    def index(self, group, step=None):
        index = 0
        for d in GROUPS[group]:
            index = index * SIZES[d] + self.coordinate(d, (step or {}).get(d, 0))[0]
        return index


def steps_of(group):
    dims = GROUPS[group]
    steps = [s for s in itertools.product(*[range(SIZES[d]) for d in dims]) if any(s)]
    return farthest_first([{d: n for d, n in zip(dims, s) if n} for s in steps])


def farthest_first(steps):
    far = {"x": 1, "y": 1, "z_lo": 1, "core": 0, "z_hi": 4}
    return sorted(steps, key=lambda step: sum(far[d] * min(n, SIZES[d] - n) for d, n in step.items()), reverse=True)


def lane_group(shape):
    return iota(shape, len(shape) - 1) // RANK


def eye_rep():
    return jnp.where(iota((RANK, 128), 0) == iota((RANK, 128), 1) % RANK, 1.0, 0.0).astype(F32)


def fold(a):
    a = a + roll(a, 64)
    return a + roll(a, 32)


def quarters_gram(h):
    g = lane_group((RANK, 128))
    t = jnp.where(g == 0, h[0:32, :], jnp.where(g == 1, h[32:64, :], jnp.where(g == 2, h[64:96, :], h[96:128, :])))
    return fold(t)


def pack_square(m):
    g = lane_group((8, 128))
    return jnp.where(g == 0, m[0:8], jnp.where(g == 1, m[8:16], jnp.where(g == 2, m[16:24], m[24:32])))


def pack_rows(m):
    g = lane_group((8, 128))
    low, high = (jnp.where(g % 2 == 1, pltpu.roll(half, 4, 0), half) for half in (m[0:8], m[8:16]))
    return jnp.where(g < 2, low, high)[0:4]


def by_quarter(m):
    g = lane_group((RANK, 128))
    return jnp.concatenate([jnp.where(g == q, m, 0.0) for q in range(4)], axis=0)


def inverse(s):
    width, block = 128, 16
    lanes, row = iota((RANK, width), 1), iota((block, width), 0)
    a = jnp.where(lanes < RANK, s, eye_rep())
    for k in range(0, RANK, block):
        columns = [jnp.broadcast_to(a[:, k + j : k + j + 1], (RANK, width)) for j in range(block)]
        rows = a[k : k + block]
        p = [column[k : k + block] for column in columns]
        for i in range(block):
            pivot = 1.0 / p[i][i : i + 1]
            here = row == i
            factor = jnp.where(here, 0.0, p[i])
            own = rows[i : i + 1] * pivot
            rows = jnp.where(here, own, rows) - factor * own
            for j in range(i + 1, block):
                own = p[j][i : i + 1] * pivot
                p[j] = jnp.where(here, own, p[j]) - factor * own
        u = columns[0] * rows[0:1]
        for j in range(1, block):
            u = u + columns[j] * rows[j : j + 1]
        pieces = [(a - u)[i : i + block] for i in range(0, RANK, block)]
        pieces[k // block] = rows
        a = jnp.concatenate(pieces, axis=0)
    return jnp.where(lanes < RANK, roll(a, 32), a)


def solver(gram_u, gram_w):
    eye = eye_rep()
    v = gram_u * gram_w
    trace = jnp.sum(jnp.sum(v * eye, axis=0, keepdims=True), axis=1, keepdims=True) / 4.0
    return inverse(v + (RIDGE_PENALTY / RANK) * trace * eye)


def scales(h, count):
    masked = h * eye_rep()
    along = 1.0 / jnp.sqrt(jnp.sum(masked, axis=0, keepdims=True) / count + EPS)
    down = 1.0 / jnp.sqrt(jnp.sum(masked, axis=1, keepdims=True) / 4.0 / count + EPS)
    return along, h * along * down / count


def kernel(tensor_hbm, b_hbm, c_hbm, a_out, b_out, c_out, w_out,
           x, c_in, b_in, y_i, y_j, x_flat, x_terms, b_send, b_rows, b_far, g_send, g_all,
           m1_send, m1_all, a_send, a_all, m2_send, m2_all, m2_half, m2_pair, m3_send, m3_parts, m3z_send, m3_z, m3_done_send, m3_done,
           hb_send, hb_far, hbx_send, hb_all, a_rows, local, sent, got, known):
    places = Places()
    at = {g: places.index(g) for g in GROUPS}
    total_i, total_j, depth = 512, 512, 256

    barrier = pltpu.get_barrier_semaphore()
    near_known, line_known, lines_known, all_known = (known.at[k] for k in range(4))
    on_core = [places.own["core"] == 0, places.own["core"] == 1]
    partner = places.device({"core": 1})

    def tell(semaphore, target):
        pl.semaphore_signal(semaphore, inc=1, device_id=target, device_id_type=MESH)

    @pl.when(on_core[0])
    def _():
        tell(barrier, partner)

    for step in steps_of("z"):
        tell(barrier, places.device(step, core=0))
    for step in steps_of("x_z") + steps_of("y"):
        tell(barrier, places.device(step, core=1))

    loads = [
        pltpu.make_async_copy(b_hbm, b_in, local.at[0]),
        pltpu.make_async_copy(c_hbm, c_in, local.at[1]),
        pltpu.make_async_copy(tensor_hbm, x, local.at[2]),
    ]
    for load in loads:
        load.start()

    rounds = itertools.count()
    pending = []

    def exchange(group, source, buffer):
        k = next(rounds)
        steps = steps_of(group)
        for step in steps:
            src = source(step) if callable(source) else source
            pltpu.make_async_remote_copy(
                src_ref=src, dst_ref=buffer.at[at[group]], send_sem=sent.at[k], recv_sem=got.at[k],
                device_id=places.device(step), device_id_type=MESH,
            ).start()
        n = len(steps)
        span = buffer.at[pl.ds(0, n)]
        return pltpu.make_async_copy(span, span, got.at[k]), pltpu.make_async_copy(span, span, sent.at[k])

    loads[0].wait()
    b4 = jnp.concatenate([b_in[...]] * 4, axis=1)
    b_send[...] = b4
    b_rows[at["row"]] = b4
    b_far[at["z"]] = b4
    loads[1].wait()
    c4 = jnp.concatenate([c_in[...]] * 4, axis=0).T
    gram_c = gram(c4)[0:32, :] / depth
    loads[2].wait()
    wide = lane_group((depth, 128))
    y = jnp.zeros((128, 128), F32)
    for q in range(4):
        part = x[:, 8 * q : 8 * q + 8, :].reshape(128, depth)
        y = y + dot(part, jnp.where(wide == q, c4, 0.0))
        x_flat[128 * q : 128 * q + 128, :] = part
    y = y.reshape(16, 8, 128)
    y_i[...] = y
    for s in range(8):
        y_j[s] = y[:, s, :]

    @pl.when(on_core[1])
    def _():
        pl.semaphore_wait(barrier, len(steps_of("row")) + 2 * len(steps_of("y")))
        tell(near_known, partner)

    @pl.when(on_core[0])
    def _():
        pl.semaphore_wait(near_known, 1)

    def go(*args):
        arrive, leave = exchange(*args)
        pending.append(leave)
        return arrive

    b_near_in = go("row", b_send, b_rows)

    @pl.when(on_core[0])
    def _():
        pl.semaphore_wait(barrier, 2 * len(steps_of("z")))
        tell(line_known, partner)
        for step in steps_of("y"):
            tell(lines_known, places.device(step))

    @pl.when(on_core[1])
    def _():
        pl.semaphore_wait(line_known, 1)

    b_far_in = go("z", b_send, b_far)

    for k, term in enumerate(split(x_flat[...])):
        x_terms[k] = term

    b_near_in.wait()
    b_pack = pack_square(b_rows[...].reshape(32, 128))
    m1 = y_j[0] * b_pack[0:1]
    for s in range(1, 8):
        m1 = m1 + y_j[s] * b_pack[s : s + 1]
    m1 = pack_rows(fold(m1))
    m1_send[...] = m1
    m1_all[at["col"]] = m1

    @pl.when(on_core[0])
    def _():
        pl.semaphore_wait(lines_known, len(steps_of("y")))
        tell(all_known, partner)

    @pl.when(on_core[1])
    def _():
        pl.semaphore_wait(all_known, 1)

    m1_in = go("col", m1_send, m1_all)

    b_far_in.wait()
    far = pack_rows(b_far[...].reshape(16, 128))
    g_send[...] = far
    g_all[at["xyc"]] = far
    g_in = go("xyc", g_send, g_all)
    m1_in.wait()
    m1 = jnp.sum(m1_all[...], axis=0)
    a_send[...] = m1
    a_all[at["row"]] = m1
    a_in = go("row", a_send, a_all)

    g_in.wait()
    gram_b = quarters_gram(gram(g_all[...].reshape(128, 128))) / total_j
    solve_a = solver(gram_b, gram_c)
    m1 = jnp.concatenate([m1, m1], axis=0)
    group8, upper = lane_group((8, 128)), iota((8, 128), 0) // 4
    m1 = jnp.concatenate([jnp.where(group8 == 2 * t + upper, m1, 0.0) for t in range(2)], axis=0)
    a_own = dot(m1, jnp.concatenate([solve_a] * 4, axis=0))
    m2 = y_i[0] * a_own[0:1]
    for i in range(1, 16):
        m2 = m2 + y_i[i] * a_own[i : i + 1]
    m2_send[...] = m2
    m2_all[at["x_z"]] = m2
    m2_in = go("x_z", m2_send, m2_all)
    a_rows[...] = a_own

    a_in.wait()
    a_every = dot(a_all[...].reshape(128, 128), by_quarter(solve_a))
    a_along, gram_a = scales(quarters_gram(gram(a_every)), total_i)

    solve_b = by_quarter(solver(gram_a, gram_c))
    m2_in.wait()
    m2 = jnp.sum(m2_all[...], axis=0)
    m2_half[...] = m2
    m2_pair[at["core"]] = m2
    m2_in = go("core", m2_half, m2_pair)

    m2_in.wait()
    b_pack = dot((m2_pair[0] + m2_pair[1]) * a_along, solve_b)
    scaled_b = b_pack * a_along
    khatri = (a_own[:, None, :] * scaled_b[None, :, :]).reshape(128, 128).T
    khatri = jnp.concatenate([khatri[32 * q : 32 * q + 32] for q in range(4)], axis=1)
    high, middle, low = split(khatri)
    first = plain_dot(jnp.concatenate([high, middle, low], axis=0), x_terms[0])
    second = plain_dot(jnp.concatenate([high, middle], axis=0), x_terms[1])
    small = first[64:96] + second[32:64] + plain_dot(high, x_terms[2])
    m3 = first[0:32] + ((first[32:64] + second[0:32]) + small)
    m3_send[...] = m3.reshape(32, 1, 256)
    m3_parts[at["xyc"]] = m3_send[at["xyc"]]
    m3_in = go("xyc", lambda step: m3_send.at[places.index("xyc", step)], m3_parts)
    own = fold(jnp.where(lane_group((8, 128)) == at["row"] // 8, b_pack, 0.0))
    own = jnp.sum(jnp.where(iota((8, 128), 0) == at["row"] % 8, own, 0.0), axis=0, keepdims=True)
    hb_send[...] = own
    hb_far[at["z"]] = own
    hb_far_in = go("z", hb_send, hb_far)
    a_out[...] = (a_rows[pl.ds(at["col"], 1), :] * a_along)[:, 0:RANK]

    m3_in.wait()
    m3 = jnp.sum(m3_parts[...], axis=0)
    m3z_send[...] = m3
    m3_z[at["z"]] = m3
    m3z_in = go("z", m3z_send, m3_z)

    hb_far_in.wait()
    hb = pack_rows(hb_far[...].reshape(16, 128))
    hbx_send[...] = hb
    hb_all[at["xyc"]] = hb
    hb_in = go("xyc", hbx_send, hb_all)

    m3z_in.wait()
    m3 = jnp.sum(m3_z[...], axis=0)
    m3_done_send[...] = m3
    m3_done[at["xyc"]] = m3
    done_in = go("xyc", m3_done_send, m3_done)

    hb_in.wait()
    b_along, gram_b = scales(quarters_gram(gram(hb_all[...].reshape(128, 128))), total_j)
    b_out[...] = (hb_send[...] * b_along)[:, 0:RANK]
    solve_c = (solver(gram_a, gram_b) * b_along)[:, 0:RANK]

    done_in.wait()
    fresh = dot(solve_c, m3_done[...].reshape(RANK, depth))
    norms = jnp.sqrt(jnp.sum(fresh * fresh, axis=1, keepdims=True) / depth + EPS)
    c_out[...] = fresh / norms
    w_out[...] = jnp.sum(norms * eye_rep(), axis=0, keepdims=True)[:, 0:RANK] / 512.0

    for leave in pending:
        leave.wait()


def hand_over(*refs):
    copies = [pltpu.make_async_copy(refs[k], refs[4 + k], refs[8].at[k]) for k in range(4)]
    for copy in copies:
        copy.start()
    for copy in copies:
        copy.wait()


def per_device(tensor, factor_b, initial_third_factor):
    tile = (8, 128)
    vmem = lambda *shape: pltpu.VMEM(shape, F32)
    results = (
        jax.ShapeDtypeStruct((1, RANK), F32),
        jax.ShapeDtypeStruct((1, RANK), F32),
        jax.ShapeDtypeStruct((RANK, 256), F32),
        jax.ShapeDtypeStruct((1, RANK), F32),
    )
    ready = pl.pallas_call(
        kernel,
        out_shape=tuple(pltpu.VMEM(r.shape, F32) for r in results),
        in_specs=[pl.BlockSpec(memory_space=pltpu.HBM)] * 3,
        out_specs=[pl.BlockSpec(memory_space=pltpu.VMEM)] * 4,
        scratch_shapes=[
            vmem(16, 32, 256), vmem(RANK, 256), vmem(1, RANK), vmem(16, *tile), vmem(8, 16, 128), vmem(512, 256), pltpu.VMEM((3, 512, 256), jnp.bfloat16),
            vmem(1, 128), vmem(32, 1, 128), vmem(16, 1, 128), vmem(4, 128), vmem(32, 4, 128),
            vmem(4, 128), vmem(16, 4, 128), vmem(4, 128), vmem(32, 4, 128),
            vmem(*tile), vmem(16, *tile), vmem(*tile), vmem(2, *tile),
            vmem(32, 1, 256), vmem(32, 1, 256), vmem(1, 256), vmem(16, 1, 256), vmem(1, 256), vmem(32, 1, 256),
            vmem(1, 128), vmem(16, 1, 128), vmem(4, 128), vmem(32, 4, 128), vmem(16, 128),
            pltpu.SemaphoreType.DMA((3,)), pltpu.SemaphoreType.DMA((12,)), pltpu.SemaphoreType.DMA((12,)),
            pltpu.SemaphoreType.REGULAR((4,)),
        ],
        compiler_params=pltpu.CompilerParams(
            collective_id=0, has_side_effects=True, vmem_limit_bytes=40 * 1024 * 1024
        ),
        name="als_sweep",
    )(*[pltpu.with_memory_space_constraint(a, pltpu.HBM) for a in (tensor, factor_b, initial_third_factor.T)])
    a, b, c, w = pl.pallas_call(
        hand_over,
        out_shape=results,
        in_specs=[pl.BlockSpec(memory_space=pltpu.VMEM)] * 4,
        out_specs=[pl.BlockSpec(memory_space=pltpu.HBM)] * 4,
        scratch_shapes=[pltpu.SemaphoreType.DMA((4,))],
        compiler_params=pltpu.CompilerParams(vmem_limit_bytes=1024 * 1024),
        name="hand_over",
    )(*ready)
    return a, b, c.T, w.reshape(RANK)


def solution(mesh):
    return jax.shard_map(
        per_device,
        mesh=mesh,
        in_specs=(P("row", "col", None), P(("col", "row"), None), P()),
        out_specs=(P(("row", "col"), None), P(("col", "row"), None), P(), P()),
        check_vma=False,
    )
```
